256 devices in a mesh: span: 16 (over y, x_hi, core), space: 16 (over x_lo, z).
Axes of the slice: x: 4 (x_hi: 2, x_lo: 2; x = x_hi * 2 + x_lo), y: 4, z: 8, core: 2. Of those that a mesh axis runs over, the one named last changes fastest.
Arguments:
- latents: bfloat16 [384, 32, 3072], P('space', 'span'), may hold values from -6 to 6
- span_order: int32 [32], replicated, may hold values from 0 to 31, each once
- modulation: float32 [32, 6, 3072], P('span'), may hold values from -2 to 10
- qkv_weight: bfloat16 [3, 3072, 2048], P(None, None, 'space'), may hold values from -0.109375 to 0.109375
- out_weight: bfloat16 [2048, 3072], P('space'), may hold values from -0.125 to 0.125
- up_weight: bfloat16 [3072, 12288], P(None, 'space'), may hold values from -0.109375 to 0.109375
- down_weight: bfloat16 [12288, 3072], P('space'), may hold values from -0.0546875 to 0.0546875
Outputs:
- mixed: bfloat16 [384, 32, 3072], P('space', 'span')
The draws below stay inside these ranges and needn't reach their ends.
Inputs may be any that keep to these rules, and one draw needn't show every extreme that they name: `span_order`: a permutation of the span places 0 to 31.
All inputs are finite; a program needn't handle non-finite values.
Results may differ from the reference program's by a relative error of at most 0.025.
The reference program's roundings to bfloat16 on the way count: a program that leaves them out, or rounds other values in their place, can miss the bound.
Values may be sent and summed in bfloat16 or wider, within the bound.
No kernel may reach another device: no remote copies, remote signals or barrier semaphores. Data moves between devices by JAX's collectives and lax.ppermute only.
A program may use at most 192 MiB of HBM per device.

```python
import jax
import jax.numpy as jnp
from jax import lax

D = 3072
HEADS = 16
HD = 128
FF = 12288
SPAN_TOK = 384
SPANS = 32
N_SPACE = 16


def draw_modulation(key, part):
    key = jax.random.fold_in(key, 11)
    first, second, third = jax.random.split(key, 3)
    shift = jnp.clip(jax.random.normal(first, (SPANS, 2, D), jnp.float32) * 0.5, -2.0, 2.0)
    scale = jax.random.uniform(second, (SPANS, 2, D), jnp.float32, -0.5, 1.0)
    gate = jax.random.uniform(third, (SPANS, 2, D), jnp.float32, 0.5, 1.5)
    return jnp.stack([shift[:, 0], scale[:, 0], gate[:, 0], shift[:, 1], scale[:, 1], gate[:, 1]], axis=1)


def level_of(own_key, dims, cuts, smallest, top_value):
    def one(axis_at, parts):
        draws = jax.random.uniform(jax.random.fold_in(jax.random.fold_in(own_key, 6), axis_at), (parts,), jnp.float32, smallest / len(cuts), top_value / len(cuts))
        return jnp.repeat(jnp.exp(draws), dims[axis_at] // parts).reshape((-1,) + (1,) * (len(dims) - axis_at - 1))

    gain = one(*cuts[0])
    for cut in cuts[1:]:
        gain = gain * one(*cut)
    return gain


def normal_values(rng, shape, scale, reach, shards=(), dtype=jnp.bfloat16):
    entries = scale * jax.random.normal(rng, shape, jnp.float32)
    if shards:
        entries = entries * level_of(rng, shape, shards, -0.22, 0.18)
    return jnp.clip(entries, -reach, reach).astype(dtype)


def setup_inputs(seed: int = 0) -> dict:
    key_list = jax.random.split(jax.random.key(seed), 8)
    latents = normal_values(key_list[0], (SPAN_TOK, SPANS, D), 1.0, 6.0, ((0, 16), (1, 16)))
    span_order = jax.random.permutation(key_list[1], SPANS).astype(jnp.int32)
    modulation = draw_modulation(jax.random.fold_in(key_list[7], 71), 0)
    qkv_weight = normal_values(key_list[3], (3, D, HEADS * HD), D ** -0.5, 0.109375, ((2, 16),))
    out_weight = normal_values(key_list[4], (HEADS * HD, D), (HEADS * HD) ** -0.5, 0.125, ((0, 16),))
    up_weight = normal_values(key_list[5], (D, FF), D ** -0.5, 0.109375, ((1, 16),))
    down_weight = normal_values(key_list[6], (FF, D), FF ** -0.5, 0.0546875, ((0, 16),))
    return {"latents": latents, "span_order": span_order, "modulation": modulation, "qkv_weight": qkv_weight, "out_weight": out_weight, "up_weight": up_weight, "down_weight": down_weight}


def norm_mod(rows, shift, scale):
    mean = lax.optimization_barrier(jnp.mean(rows, axis=-1, keepdims=True))
    centred = rows - mean
    variance = lax.optimization_barrier(jnp.mean(centred * centred, axis=-1, keepdims=True))
    return (centred * lax.rsqrt(variance + 1e-06) * (1.0 + scale) + shift).astype(jnp.bfloat16)

def grouped_sum(left, right, groups):
    width = left.shape[1] // groups
    total = jnp.zeros((left.shape[0], right.shape[1]), jnp.float32)
    for group in range(groups):
        part = jnp.dot(left[:, group * width:(group + 1) * width], right[group * width:(group + 1) * width], preferred_element_type=jnp.float32)
        total = total + lax.optimization_barrier(part.astype(jnp.bfloat16)).astype(jnp.float32)
    return total

def reference(latents, span_order, modulation, qkv_weight, out_weight, up_weight, down_weight):
    rows_f = latents.astype(jnp.float32)
    normed = norm_mod(rows_f, modulation[None, :, 0], modulation[None, :, 1])
    projected = jnp.einsum('tcd,sdf->stcf', normed.astype(jnp.float32), qkv_weight.astype(jnp.float32)).astype(jnp.bfloat16)
    per_head = projected.reshape(3, SPAN_TOK, SPANS, HEADS, HD).transpose(3, 0, 2, 1, 4)
    factor = 1.0 / HD ** 0.5

    def one_head(stacked):
        query = stacked[0].astype(jnp.float32)
        keys = stacked[1].astype(jnp.float32)
        values = stacked[2].astype(jnp.float32)

        def one_span(item):
            block, place = item
            scores = jnp.einsum('td,bud->tbu', block, keys) * factor
            allowed = (span_order <= place)[None, :, None]
            scores = jnp.where(allowed, scores, -1e+30)
            peak = lax.optimization_barrier(jnp.max(scores, axis=(1, 2), keepdims=True))
            expo = jnp.where(allowed, jnp.exp(scores - peak), 0.0)
            total = lax.optimization_barrier(jnp.sum(expo, axis=(1, 2)))
            weights = expo.astype(jnp.bfloat16).astype(jnp.float32)
            return jnp.einsum('tbu,bud->td', weights, values) / total[:, None]
        return lax.map(one_span, (query, span_order))
    heads_out = lax.map(one_head, per_head)
    attended = heads_out.transpose(2, 1, 0, 3).reshape(SPAN_TOK * SPANS, HEADS * HD).astype(jnp.bfloat16)
    attn_sum = grouped_sum(attended, out_weight, N_SPACE).reshape(SPAN_TOK, SPANS, D)
    residual = (rows_f + modulation[None, :, 2] * attn_sum).astype(jnp.bfloat16)
    second = norm_mod(residual.astype(jnp.float32), modulation[None, :, 3], modulation[None, :, 4])
    hidden = jax.nn.gelu(jnp.dot(second.reshape(-1, D), up_weight, preferred_element_type=jnp.float32), approximate=True).astype(jnp.bfloat16)
    ffn_sum = grouped_sum(hidden, down_weight, N_SPACE).reshape(SPAN_TOK, SPANS, D)
    return (residual.astype(jnp.float32) + modulation[None, :, 5] * ffn_sum).astype(jnp.bfloat16)
```

```python
import functools

import jax
import jax.numpy as jnp
from jax import lax
from jax.experimental import pallas as pl
from jax.experimental.pallas import tpu as pltpu
from jax.sharding import PartitionSpec as P

HD = 128
Y, X, CORES, Z = 4, 4, 2, 8
AXES = ("span", "space")


def norm_mod(rows, shift, scale):
    mean = jnp.mean(rows, axis=-1, keepdims=True)
    centred = rows - mean
    variance = jnp.mean(centred * centred, axis=-1, keepdims=True)
    return (centred * lax.rsqrt(variance + 1e-06) * (1.0 + scale) + shift).astype(jnp.bfloat16)


def number(y, x, core, z):
    return (((y % Y) * 2 + (x % X) // 2) * CORES + core) * 16 + (x % X) % 2 * Z + z % Z


def send(value, move):
    pairs = []
    for y in range(Y):
        for x in range(X):
            for core in range(CORES):
                for z in range(Z):
                    pairs.append((number(y, x, core, z), number(*move(y, x, core, z))))
    return lax.ppermute(value, AXES, pairs)


def z_pair(y, x, core, z):
    return y, x, core, z ^ 1


def z_cross(y, x, core, z):
    return y, x, core, (z + 1 if z % 2 else z - 1)


def x_pair(y, x, core, z):
    return y, x ^ 1, core, z


def x_cross(y, x, core, z):
    return y, (x + 1 if x % 2 else x - 1), core, z


def x_two(y, x, core, z):
    return y, x + 2, core, z


def x_lane(y, x, core, z):
    return (x_pair if core == 0 else x_cross)(y, x, core, z)


def other_core(y, x, core, z):
    return y, x, 1 - core, z


def y_pair(y, x, core, z):
    return y ^ 1, x, core, z


def y_cross(y, x, core, z):
    return (y + 1 if y % 2 else y - 1), x, core, z


def y_lane(y, x, core, z):
    return (y_pair if core == 0 else y_cross)(y, x, core, z)


def y_lane_back(y, x, core, z):
    return (y_cross if core == 0 else y_pair)(y, x, core, z)


hold = lax.optimization_barrier


def stage(sends, rider=None):
    if rider is not None:
        moves = [move for _, move in sends] + [rider[1]]
        values = hold(tuple(value for value, _ in sends) + (rider[0],))
        sends = list(zip(values, moves))
    return hold(tuple(send(value, move) for value, move in sends))


def gather_z(mine):
    own = near0 = far0 = mine[:1]
    own1 = near1 = far1 = mine[1:]
    chain0, chain1 = [own], [own1]
    for _ in range(3):
        near0, far0, near1, far1 = stage(
            [(far0, z_pair), (near0, z_cross), (far1, z_pair), (near1, z_cross)]
        )
        chain0 += [near0, far0]
        chain1 += [near1, far1]
    last0, last1 = stage([(far0, z_pair), (near1, z_cross)])
    return [jnp.concatenate(both, 0) for both in zip(chain0 + [last0], chain1 + [last1])]


def plus(a, b):
    return (a.astype(jnp.float32) + b.astype(jnp.float32)).astype(jnp.bfloat16)


def scatter_sum_z(blocks, riders=(None,) * 4):
    first = [b[:1] for b in blocks]
    second = [b[1:] for b in blocks]
    pair0, cross1, *carried = stage([(first[7], z_pair), (second[7], z_cross)], riders[0])
    pair0, cross0, pair1, cross1, *more = stage(
        [
            (first[5], z_pair),
            (plus(first[6], pair0), z_cross),
            (plus(second[5], cross1), z_pair),
            (second[6], z_cross),
        ],
        riders[1],
    )
    carried += more
    for at, rider in ((3, riders[2]), (1, riders[3])):
        pair0, cross0, pair1, cross1, *more = stage(
            [
                (plus(first[at], cross0), z_pair),
                (plus(first[at + 1], pair0), z_cross),
                (plus(second[at], cross1), z_pair),
                (plus(second[at + 1], pair1), z_cross),
            ],
            rider,
        )
        carried += more
    total0 = first[0].astype(jnp.float32) + pair0.astype(jnp.float32) + cross0.astype(jnp.float32)
    total1 = second[0].astype(jnp.float32) + pair1.astype(jnp.float32) + cross1.astype(jnp.float32)
    return jnp.concatenate([total0, total1], 0), carried


def norm_kernel(rows, modulation, out):
    for span in range(rows.shape[0]):
        shift, scale = modulation[span, 0:1, :], modulation[span, 1:2, :]
        out[span] = norm_mod(rows[span].astype(jnp.float32), shift, scale)


def norm_rows(rows, modulation):
    vmem = pl.BlockSpec(memory_space=pltpu.VMEM)
    return pl.pallas_call(
        norm_kernel,
        out_shape=jax.ShapeDtypeStruct(rows.shape, jnp.bfloat16),
        in_specs=[vmem, vmem],
        out_specs=vmem,
    )(rows, modulation)


def attend_kernel(last, first, key_places, query_places, query, piece, *rest):
    if not first:
        peak_in, total_in, accum_in = rest[:3]
        rest = rest[3:]
    if last:
        out, peak, total, accum, held = rest
    else:
        peak, total, accum, held = rest
    spans = query.shape[0]
    if first:
        peak[...] = jnp.full(peak.shape, -1e30, jnp.float32)
        total[...] = jnp.zeros(total.shape, jnp.float32)
        accum[...] = jnp.zeros(accum.shape, jnp.float32)
    else:
        peak[...] = peak_in[...]
        total[...] = total_in[...]
        accum[...] = accum_in[...]
    factor = 1.4426950408889634 / HD**0.5
    count, width, _ = piece.shape

    def score(span, block):
        return lax.dot_general(
            query[span],
            piece[block, :, :HD],
            (((1,), (1,)), ((), ())),
            preferred_element_type=jnp.float32,
        )

    for span in range(spans):
        held[0, span] = score(span, 0)

    def two_blocks(pair, carry):
        for slot in range(2):
            block = 2 * pair + slot
            following = jnp.minimum(block + 1, count - 1)
            values = piece[block, :, HD:]
            for span in range(spans):
                held[1 - slot, span] = score(span, following)
                scores = held[slot, span]
                seen = key_places[block] <= query_places[span]
                old = peak[span]
                top = jnp.max(scores, axis=1, keepdims=True)
                new = jnp.where(seen, jnp.maximum(old, top), old)
                guard = jnp.where(seen, new, 1e30)
                wide = jnp.concatenate([guard] * (width // HD), axis=1)
                expo = jnp.exp2((scores - wide) * factor)
                shrink = jnp.exp2((old - new) * factor)
                part = expo[:, :HD]
                for lane in range(HD, width, HD):
                    part = part + expo[:, lane : lane + HD]
                peak[span] = new
                total[span] = total[span] * shrink + part
                accum[span] = accum[span] * shrink + jnp.dot(
                    expo.astype(jnp.bfloat16), values, preferred_element_type=jnp.float32
                )
        return carry

    lax.fori_loop(0, count // 2, two_blocks, 0)
    if last:
        for span in range(spans):
            whole = jnp.sum(total[span], axis=1, keepdims=True)
            out[span] = (accum[span] / whole).astype(jnp.bfloat16)


def attend(key_places, query_places, query, piece, state, last=False):
    spans, rows, _ = query.shape
    count, width, _ = piece.shape
    wide = jax.ShapeDtypeStruct((spans, rows, HD), jnp.float32)
    smem = pl.BlockSpec(memory_space=pltpu.SMEM)
    vmem = pl.BlockSpec(memory_space=pltpu.VMEM)
    scratch = [pltpu.VMEM((spans, rows, HD), jnp.float32)] * 3 if last else []
    work = 4 * spans * rows * HD * count * width
    return pl.pallas_call(
        functools.partial(attend_kernel, last, state is None),
        out_shape=jax.ShapeDtypeStruct((spans, rows, HD), jnp.bfloat16) if last else (wide,) * 3,
        in_specs=[smem, smem, vmem, vmem] + [vmem] * (0 if state is None else 3),
        out_specs=vmem if last else (vmem,) * 3,
        scratch_shapes=scratch + [pltpu.VMEM((2, spans, rows, width), jnp.float32)],
        compiler_params=pltpu.CompilerParams(vmem_limit_bytes=24 * 1024 * 1024),
        cost_estimate=pl.CostEstimate(
            flops=work, bytes_accessed=4 * 1024 * 1024, transcendentals=work // (4 * HD)
        ),
    )(key_places, query_places, query, piece, *(() if state is None else state))


def body(latents, span_order, modulation, qkv_weight, out_weight, up_weight, down_weight):
    place = lax.axis_index("span")
    core, xh, y = place % 2, place // 2 % 2, place // 4
    stored = latents.transpose(1, 0, 2)
    rows = stored.astype(jnp.float32)
    gate1, shift2, scale2, gate2 = (modulation[:, None, i] for i in range(2, 6))

    depth = qkv_weight.shape[1] // 2
    qkv_mine = send(lax.dynamic_slice_in_dim(qkv_weight, core * depth, depth, 1), x_lane)
    out_other = send(out_weight, x_lane)
    qkv_rest = send(qkv_mine, other_core)
    normed = jnp.concatenate(gather_z(norm_rows(stored, modulation)), 1)
    qkv_other = jnp.concatenate(
        [jnp.where(core == 0, qkv_mine, qkv_rest), jnp.where(core == 0, qkv_rest, qkv_mine)], 1
    )
    qkv_other, out_other = hold((qkv_other, out_other))

    def project(weight):
        return jnp.einsum(
            "jtd,sdf->sjtf", normed, weight, preferred_element_type=jnp.float32
        ).astype(jnp.bfloat16)

    query1, key1, value1 = project(qkv_other)
    got_pair = send(jnp.concatenate([key1, value1, query1], -1), x_pair)
    got_cross = send(jnp.concatenate([key1, value1], -1), x_cross)
    query0, key0, value0 = project(qkv_weight)
    both0 = jnp.concatenate([key0, value0], -1)
    got_two = send(both0, x_two)
    query = jnp.concatenate([query0, got_pair[..., 2 * HD :]], 1)
    piece = jnp.concatenate(
        [
            jnp.concatenate([both0, got_pair[..., : 2 * HD]], 1),
            jnp.concatenate([got_two, got_cross], 1),
        ],
        0,
    )
    half = up_weight.shape[1] // 2
    up_from, piece = hold((up_weight, piece))
    up_mine = send(lax.dynamic_slice_in_dim(up_from, core * half, half, 1), x_lane)

    def places(at_y, at_core):
        own = 2 * (4 * (at_y % Y) + 2 * xh + at_core)
        far = 2 * (4 * (at_y % Y) + 2 * (1 - xh) + at_core)
        return jnp.concatenate(
            [lax.dynamic_slice_in_dim(span_order, own, 2), lax.dynamic_slice_in_dim(span_order, far, 2)]
        )

    def chip_places(at_y, at_core):
        return jnp.concatenate([places(at_y, at_core), places(at_y, 1 - at_core)])

    mine = lax.dynamic_slice_in_dim(span_order, 2 * place, 2)
    pair_y, cross_y = y + 1 - 2 * (y % 2), y - 1 + 2 * (y % 2) + Y
    near_y = jnp.where(core == 0, pair_y, cross_y)
    next_y = jnp.where(core == 0, cross_y, pair_y)
    tables = hold(
        (
            mine,
            chip_places(y, core),
            chip_places(near_y, core),
            chip_places(next_y, 1 - core),
            places(y + 2, core),
            places(y + 2, 1 - core),
            piece,
        )
    )
    mine, here_at, near_at, next_at, far_at, rest_at, piece = tables
    chip = jnp.concatenate([piece, send(piece, other_core)], 0)
    near = send(chip, y_lane)
    state = attend(here_at, mine, query, chip, None)
    near, state = hold((near, state))
    far = send(near[: piece.shape[0]], y_lane_back)
    near_rest = send(near, other_core)
    state = attend(near_at, mine, query, near, state)
    near_rest, state = hold((near_rest, state))
    state = attend(next_at, mine, query, near_rest, state)
    far, state, up_mine = hold((far, state, up_mine))
    far_rest = send(far, other_core)
    state = attend(far_at, mine, query, far, state)
    attended = attend(rest_at, mine, query, far_rest, state, True)
    tokens = attended.shape[1] // 2
    attended = jnp.concatenate([attended[:, :tokens], send(attended[:, tokens:], x_pair)], -1)
    part = jnp.einsum(
        "jtk,kd->jtd",
        attended,
        jnp.concatenate([out_weight, out_other], 0),
        preferred_element_type=jnp.float32,
    ).astype(jnp.bfloat16)
    part, up_mine, down_from = hold((part, up_mine, down_weight))
    up_rest = send(up_mine, other_core)
    quarter = half // 4
    riders = [
        (lax.dynamic_slice_in_dim(down_from, core * half + quarter * i, quarter, 0), x_lane)
        for i in range(4)
    ]
    attn_sum, carried = scatter_sum_z(jnp.split(part, Z, 1), riders)
    down_mine = jnp.concatenate(carried, 0)
    down_rest = send(down_mine, other_core)
    residual = (rows + gate1 * attn_sum).astype(jnp.bfloat16)
    second = gather_z(norm_mod(residual.astype(jnp.float32), shift2, scale2))
    down_all = jnp.concatenate([down_weight, down_mine, down_rest], 0)

    def feed(blocks):
        tokens = jnp.concatenate(blocks, 1)
        hidden = jnp.concatenate(
            [
                jax.nn.gelu(
                    jnp.einsum("jtd,df->jtf", tokens, up, preferred_element_type=jnp.float32),
                    approximate=True,
                ).astype(jnp.bfloat16)
                for up in (up_weight, up_mine, up_rest)
            ],
            -1,
        )
        part = jnp.einsum(
            "jtf,fd->jtd", hold(hidden), hold(down_all), preferred_element_type=jnp.float32
        ).astype(jnp.bfloat16)
        return jnp.split(part, len(blocks), 1)

    ffn_sum, _ = scatter_sum_z(feed(second[:5]) + feed(second[5:]))
    mixed = residual.astype(jnp.float32) + gate2 * ffn_sum
    return mixed.astype(jnp.bfloat16).transpose(1, 0, 2)


def solution(mesh):
    return jax.shard_map(
        body,
        mesh=mesh,
        in_specs=(
            P("space", "span", None),
            P(),
            P("span", None, None),
            P(None, None, "space"),
            P("space", None),
            P(None, "space"),
            P("space", None),
        ),
        out_specs=P("space", "span", None),
        check_vma=False,
    )
```

```python
import functools

import jax
import jax.numpy as jnp
from jax import lax
from jax.experimental import pallas as pl
from jax.experimental.pallas import tpu as pltpu
from jax.sharding import PartitionSpec as P

HD = 128
Y, X, CORES, Z = 4, 4, 2, 8
AXES = ("span", "space")


def norm_mod(rows, shift, scale):
    mean = jnp.mean(rows, axis=-1, keepdims=True)
    centred = rows - mean
    variance = jnp.mean(centred * centred, axis=-1, keepdims=True)
    return (centred * lax.rsqrt(variance + 1e-06) * (1.0 + scale) + shift).astype(jnp.bfloat16)


def number(y, x, core, z):
    return (((y % Y) * 2 + (x % X) // 2) * CORES + core) * 16 + (x % X) % 2 * Z + z % Z


def send(value, move):
    pairs = []
    for y in range(Y):
        for x in range(X):
            for core in range(CORES):
                for z in range(Z):
                    pairs.append((number(y, x, core, z), number(*move(y, x, core, z))))
    return lax.ppermute(value, AXES, pairs)


def z_pair(y, x, core, z):
    return y, x, core, z ^ 1


def z_cross(y, x, core, z):
    return y, x, core, (z + 1 if z % 2 else z - 1)


def x_pair(y, x, core, z):
    return y, x ^ 1, core, z


def x_cross(y, x, core, z):
    return y, (x + 1 if x % 2 else x - 1), core, z


def x_two(y, x, core, z):
    return y, x + 2, core, z


def x_lane(y, x, core, z):
    return (x_pair if core == 0 else x_cross)(y, x, core, z)


def other_core(y, x, core, z):
    return y, x, 1 - core, z


def y_pair(y, x, core, z):
    return y ^ 1, x, core, z


def y_cross(y, x, core, z):
    return (y + 1 if y % 2 else y - 1), x, core, z


def y_lane(y, x, core, z):
    return (y_pair if core == 0 else y_cross)(y, x, core, z)


def y_lane_back(y, x, core, z):
    return (y_cross if core == 0 else y_pair)(y, x, core, z)


hold = lax.optimization_barrier


def gather_z(own, rider=None):
    near = far = own
    blocks = [own]
    for step in range(3):
        near, far = send(far, z_pair), send(near, z_cross)
        if step == 1 and rider is not None:
            near, far, rider = hold((near, far, rider))
        blocks += [near, far]
    last = jnp.concatenate([send(far[:1], z_pair), send(near[1:], z_cross)], 0)
    blocks.append(last)
    return blocks if rider is None else (blocks, rider)


def plus(a, b):
    return (a.astype(jnp.float32) + b.astype(jnp.float32)).astype(jnp.bfloat16)


def scatter_sum_z(blocks, rider=None):
    own, near1, far1, near2, far2, near3, far3, last = blocks
    pair, cross = send(last[:1], z_pair), send(last[1:], z_cross)
    near3 = jnp.concatenate([near3[:1], plus(near3[1:], cross)], 0)
    far3 = jnp.concatenate([plus(far3[:1], pair), far3[1:]], 0)
    pair, cross = send(near3, z_pair), send(far3, z_cross)
    if rider is not None:
        pair, cross, rider = hold((pair, cross, rider))
    pair, cross = send(plus(near2, cross), z_pair), send(plus(far2, pair), z_cross)
    pair, cross = send(plus(near1, cross), z_pair), send(plus(far1, pair), z_cross)
    total = own.astype(jnp.float32) + pair.astype(jnp.float32) + cross.astype(jnp.float32)
    return total if rider is None else (total, rider)


def norm_kernel(rows, modulation, out):
    for span in range(out.shape[0]):
        shift, scale = modulation[0, span : span + 1, :], modulation[1, span : span + 1, :]
        out[span] = norm_mod(rows[:, span, :].astype(jnp.float32), shift, scale)


def norm_rows(rows, modulation):
    vmem = pl.BlockSpec(memory_space=pltpu.VMEM)
    tokens, spans, width = rows.shape
    return pl.pallas_call(
        norm_kernel,
        out_shape=jax.ShapeDtypeStruct((spans, tokens, width), jnp.bfloat16),
        in_specs=[vmem, vmem],
        out_specs=vmem,
    )(rows, modulation.transpose(1, 0, 2))


def attend_kernel(n_pieces, last, first, key_places, query_places, query, *rest):
    pieces, rest = rest[:n_pieces], rest[n_pieces:]
    if not first:
        peak_in, total_in, accum_in = rest[:3]
        rest = rest[3:]
    if last:
        out, peak, total, accum, held = rest
    else:
        peak, total, accum, held = rest
    spans = query.shape[0]
    if first:
        peak[...] = jnp.full(peak.shape, -1e30, jnp.float32)
        total[...] = jnp.zeros(total.shape, jnp.float32)
        accum[...] = jnp.zeros(accum.shape, jnp.float32)
    else:
        peak[...] = peak_in[...]
        total[...] = total_in[...]
        accum[...] = accum_in[...]
    factor = 1.4426950408889634 / HD**0.5
    count, width, _ = pieces[0].shape

    def score(piece, span, block):
        return lax.dot_general(
            query[span],
            piece[block, :, :HD],
            (((1,), (1,)), ((), ())),
            preferred_element_type=jnp.float32,
        )

    def two_blocks(number, piece, pair):
        for slot in range(2):
            block = 2 * pair + slot
            following = jnp.minimum(block + 1, count - 1)
            values = piece[block, :, HD:]
            for span in range(spans):
                held[1 - slot, span] = score(piece, span, following)
                scores = held[slot, span]
                seen = key_places[number * count + block] <= query_places[span]
                old = peak[span]
                top = jnp.max(scores, axis=1, keepdims=True)
                new = jnp.where(seen, jnp.maximum(old, top), old)
                guard = jnp.where(seen, new, 1e30)
                wide = jnp.concatenate([guard] * (width // HD), axis=1)
                expo = jnp.exp2((scores - wide) * factor)
                shrink = jnp.exp2((old - new) * factor)
                part = expo[:, :HD]
                for lane in range(HD, width, HD):
                    part = part + expo[:, lane : lane + HD]
                peak[span] = new
                total[span] = total[span] * shrink + part
                accum[span] = accum[span] * shrink + jnp.dot(
                    expo.astype(jnp.bfloat16), values, preferred_element_type=jnp.float32
                )

    for number, piece in enumerate(pieces):
        for span in range(spans):
            held[0, span] = score(piece, span, 0)

        def step(pair, carry, number=number, piece=piece):
            two_blocks(number, piece, pair)
            return carry

        lax.fori_loop(0, count // 2, step, 0)
    if last:
        for span in range(spans):
            whole = jnp.sum(total[span], axis=1, keepdims=True)
            out[span] = (accum[span] / whole).astype(jnp.bfloat16)


def attend(key_places, query_places, query, pieces, state, last=False):
    spans, rows, _ = query.shape
    count, width, _ = pieces[0].shape
    wide = jax.ShapeDtypeStruct((spans, rows, HD), jnp.float32)
    smem = pl.BlockSpec(memory_space=pltpu.SMEM)
    vmem = pl.BlockSpec(memory_space=pltpu.VMEM)
    scratch = [pltpu.VMEM((spans, rows, HD), jnp.float32)] * 3 if last else []
    return pl.pallas_call(
        functools.partial(attend_kernel, len(pieces), last, state is None),
        out_shape=jax.ShapeDtypeStruct((spans, rows, HD), jnp.bfloat16) if last else (wide,) * 3,
        in_specs=[smem, smem, vmem] + [vmem] * (len(pieces) + (0 if state is None else 3)),
        out_specs=vmem if last else (vmem,) * 3,
        scratch_shapes=scratch + [pltpu.VMEM((2, spans, rows, width), jnp.float32)],
        compiler_params=pltpu.CompilerParams(vmem_limit_bytes=24 * 1024 * 1024),
        cost_estimate=pl.CostEstimate(flops=1000, bytes_accessed=1000, transcendentals=0),
    )(key_places, query_places, query, *pieces, *(() if state is None else state))


def body(latents, span_order, modulation, qkv_weight, out_weight, up_weight, down_weight):
    place = lax.axis_index("span")
    core, xh, y = place % 2, place // 2 % 2, place // 4
    rows = latents.astype(jnp.float32).transpose(1, 0, 2)
    gate1, shift2, scale2, gate2 = (modulation[:, None, i] for i in range(2, 6))

    depth = qkv_weight.shape[1] // 2
    qkv_mine = send(lax.dynamic_slice_in_dim(qkv_weight, core * depth, depth, 1), x_lane)
    out_other = send(out_weight, x_lane)
    qkv_rest = send(qkv_mine, other_core)
    normed = gather_z(norm_rows(latents, modulation))
    normed = [jnp.concatenate(normed[:5], 1), jnp.concatenate(normed[5:], 1)]
    qkv_other = jnp.concatenate(
        [jnp.where(core == 0, qkv_mine, qkv_rest), jnp.where(core == 0, qkv_rest, qkv_mine)], 1
    )
    qkv_other, out_other = hold((qkv_other, out_other))

    def project(weight):
        parts = [
            jnp.einsum("jtd,sdf->sjtf", tokens, weight, preferred_element_type=jnp.float32)
            for tokens in normed
        ]
        return jnp.concatenate([part.astype(jnp.bfloat16) for part in parts], 2)

    query1, key1, value1 = project(qkv_other)
    got_pair = send(jnp.concatenate([key1, value1, query1], -1), x_pair)
    got_cross = send(jnp.concatenate([key1, value1], -1), x_cross)
    query0, key0, value0 = project(qkv_weight)
    both0 = jnp.concatenate([key0, value0], -1)
    got_two = send(both0, x_two)
    query = jnp.concatenate([query0, got_pair[..., 2 * HD :]], 1)
    piece = jnp.concatenate(
        [
            jnp.concatenate([both0, got_pair[..., : 2 * HD]], 1),
            jnp.concatenate([got_two, got_cross], 1),
        ],
        0,
    )
    half = up_weight.shape[1] // 2
    up_from, piece = hold((up_weight, piece))
    up_mine = send(lax.dynamic_slice_in_dim(up_from, core * half, half, 1), x_lane)

    def places(at_y, at_core):
        own = 2 * (4 * (at_y % Y) + 2 * xh + at_core)
        far = 2 * (4 * (at_y % Y) + 2 * (1 - xh) + at_core)
        return jnp.concatenate(
            [lax.dynamic_slice_in_dim(span_order, own, 2), lax.dynamic_slice_in_dim(span_order, far, 2)]
        )

    mine = lax.dynamic_slice_in_dim(span_order, 2 * place, 2)
    pair_y, cross_y = y + 1 - 2 * (y % 2), y - 1 + 2 * (y % 2) + Y
    near_y = jnp.where(core == 0, pair_y, cross_y)
    next_y = jnp.where(core == 0, cross_y, pair_y)
    here_at, first_at, second_at, far_at, rest_at, mine, piece = hold(
        (
            jnp.concatenate([places(y, core), places(y, 1 - core)]),
            jnp.concatenate([places(near_y, core), places(next_y, 1 - core)]),
            jnp.concatenate([places(near_y, 1 - core), places(next_y, core)]),
            places(y + 2, core),
            places(y + 2, 1 - core),
            mine,
            piece,
        )
    )
    near = send(piece, y_lane)
    beside = send(piece, other_core)
    near_beside = send(beside, y_lane)
    state = attend(here_at, mine, query, [piece, beside], None)
    near, near_beside, state = hold((near, near_beside, state))
    far = send(near, y_lane_back)
    near_rest, beside_rest = send(near, other_core), send(near_beside, other_core)
    state = attend(first_at, mine, query, [near, near_rest], state)
    state = attend(second_at, mine, query, [near_beside, beside_rest], state)
    far, state, up_mine, down_from = hold((far, state, up_mine, down_weight))
    far_rest = send(far, other_core)
    state = attend(far_at, mine, query, [far], state)
    attended = attend(rest_at, mine, query, [far_rest], state, True)
    tokens = attended.shape[1] // 2
    attended = jnp.concatenate([attended[:, :tokens], send(attended[:, tokens:], x_pair)], -1)
    part = jnp.einsum(
        "jtk,kd->jtd",
        attended,
        jnp.concatenate([out_weight, out_other], 0),
        preferred_element_type=jnp.float32,
    ).astype(jnp.bfloat16)
    up_rest = send(up_mine, other_core)
    quarter = half // 2
    down_first = lax.dynamic_slice_in_dim(down_from, core * half, quarter, 0)
    down_first = send(down_first, x_lane)
    attn_sum, down_first = scatter_sum_z(jnp.split(part, Z, 1), down_first)
    down_from, down_first = hold((down_from, down_first))
    down_second = lax.dynamic_slice_in_dim(down_from, core * half + quarter, quarter, 0)
    down_second = send(down_second, x_lane)
    residual = (rows + gate1 * attn_sum).astype(jnp.bfloat16)
    second = norm_mod(residual.astype(jnp.float32), shift2, scale2)
    second, down_second = gather_z(second, down_second)
    down_mine = jnp.concatenate([down_first, down_second], 0)
    down_rest = send(down_mine, other_core)

    def feed(blocks):
        tokens = jnp.concatenate(blocks, 1)
        part = None
        for up, down in ((up_weight, down_weight), (up_mine, down_mine), (up_rest, down_rest)):
            hidden = jax.nn.gelu(
                jnp.einsum("jtd,df->jtf", tokens, up, preferred_element_type=jnp.float32),
                approximate=True,
            ).astype(jnp.bfloat16)
            more = jnp.einsum("jtf,fd->jtd", hold(hidden), down, preferred_element_type=jnp.float32)
            part = more if part is None else part + more
        part = part.astype(jnp.bfloat16)
        return jnp.split(part, len(blocks), 1)

    ffn_sum = scatter_sum_z(feed(second[:5]) + feed(second[5:]))
    mixed = residual.astype(jnp.float32) + gate2 * ffn_sum
    return mixed.astype(jnp.bfloat16).transpose(1, 0, 2)


def solution(mesh):
    return jax.shard_map(
        body,
        mesh=mesh,
        in_specs=(
            P("space", "span", None),
            P(),
            P("span", None, None),
            P(None, None, "space"),
            P("space", None),
            P(None, "space"),
            P("space", None),
        ),
        out_specs=P("space", "span", None),
        check_vma=False,
    )
```

```python
import functools

import jax
import jax.numpy as jnp
from jax import lax
from jax.experimental import pallas as pl
from jax.experimental.pallas import tpu as pltpu
from jax.sharding import PartitionSpec as P

HD = 128
Y, X, CORES, Z = 4, 4, 2, 8
AXES = ("span", "space")


def norm_mod(rows, shift, scale):
    mean = jnp.mean(rows, axis=-1, keepdims=True)
    centred = rows - mean
    variance = jnp.mean(centred * centred, axis=-1, keepdims=True)
    return (centred * lax.rsqrt(variance + 1e-06) * (1.0 + scale) + shift).astype(jnp.bfloat16)


def number(y, x, core, z):
    return (((y % Y) * 2 + (x % X) // 2) * CORES + core) * 16 + (x % X) % 2 * Z + z % Z


def send(value, move):
    pairs = []
    for y in range(Y):
        for x in range(X):
            for core in range(CORES):
                for z in range(Z):
                    pairs.append((number(y, x, core, z), number(*move(y, x, core, z))))
    return lax.ppermute(value, AXES, pairs)


def z_pair(y, x, core, z):
    return y, x, core, z ^ 1


def z_cross(y, x, core, z):
    return y, x, core, (z + 1 if z % 2 else z - 1)


def x_pair(y, x, core, z):
    return y, x ^ 1, core, z


def x_cross(y, x, core, z):
    return y, (x + 1 if x % 2 else x - 1), core, z


def x_two(y, x, core, z):
    return y, x + 2, core, z


def x_lane(y, x, core, z):
    return (x_pair if core == 0 else x_cross)(y, x, core, z)


def other_core(y, x, core, z):
    return y, x, 1 - core, z


def y_pair(y, x, core, z):
    return y ^ 1, x, core, z


def y_cross(y, x, core, z):
    return (y + 1 if y % 2 else y - 1), x, core, z


def y_lane(y, x, core, z):
    return (y_pair if core == 0 else y_cross)(y, x, core, z)


def y_lane_back(y, x, core, z):
    return (y_cross if core == 0 else y_pair)(y, x, core, z)


hold = lax.optimization_barrier


def gather_z(mine):
    chains = []
    for span in range(2):
        near = far = mine[span : span + 1]
        blocks = [near]
        for _ in range(3):
            near, far = send(far, z_pair), send(near, z_cross)
            blocks += [near, far]
        blocks.append(send(far, z_pair) if span == 0 else send(near, z_cross))
        chains.append(blocks)
    return [jnp.concatenate(both, 0) for both in zip(*chains)]


def plus(a, b):
    return (a.astype(jnp.float32) + b.astype(jnp.float32)).astype(jnp.bfloat16)


def scatter_sum_z(blocks, rider=None):
    own, near1, far1, near2, far2, near3, far3, last = blocks
    pair, cross = hold((send(last[:1], z_pair), send(last[1:], z_cross)))
    near3 = jnp.concatenate([near3[:1], plus(near3[1:], cross)], 0)
    far3 = jnp.concatenate([plus(far3[:1], pair), far3[1:]], 0)
    pair, cross = hold((send(near3, z_pair), send(far3, z_cross)))
    pair, cross = send(plus(near2, cross), z_pair), send(plus(far2, pair), z_cross)
    if rider is None:
        pair, cross = hold((pair, cross))
    else:
        pair, cross, rider = hold((pair, cross, rider))
    pair, cross = send(plus(near1, cross), z_pair), send(plus(far1, pair), z_cross)
    total = own.astype(jnp.float32) + pair.astype(jnp.float32) + cross.astype(jnp.float32)
    return total if rider is None else (total, rider)


def norm_kernel(rows, modulation, out):
    for span in range(out.shape[0]):
        shift, scale = modulation[0, span : span + 1, :], modulation[1, span : span + 1, :]
        out[span] = norm_mod(rows[:, span, :].astype(jnp.float32), shift, scale)


def norm_rows(rows, modulation):
    vmem = pl.BlockSpec(memory_space=pltpu.VMEM)
    tokens, spans, width = rows.shape
    return pl.pallas_call(
        norm_kernel,
        out_shape=jax.ShapeDtypeStruct((spans, tokens, width), jnp.bfloat16),
        in_specs=[vmem, vmem],
        out_specs=vmem,
    )(rows, modulation.transpose(1, 0, 2))


def attend_kernel(n_pieces, last, first, key_places, query_places, query, *rest):
    pieces, rest = rest[:n_pieces], rest[n_pieces:]
    if not first:
        peak_in, total_in, accum_in = rest[:3]
        rest = rest[3:]
    if last:
        out, peak, total, accum, held = rest
    else:
        peak, total, accum, held = rest
    spans = query.shape[0]
    if first:
        peak[...] = jnp.full(peak.shape, -1e30, jnp.float32)
        total[...] = jnp.zeros(total.shape, jnp.float32)
        accum[...] = jnp.zeros(accum.shape, jnp.float32)
    else:
        peak[...] = peak_in[...]
        total[...] = total_in[...]
        accum[...] = accum_in[...]
    factor = 1.4426950408889634 / HD**0.5
    count, width, _ = pieces[0].shape

    def score(piece, span, block):
        return lax.dot_general(
            query[span],
            piece[block, :, :HD],
            (((1,), (1,)), ((), ())),
            preferred_element_type=jnp.float32,
        )

    def two_blocks(number, piece, pair):
        for slot in range(2):
            block = 2 * pair + slot
            following = jnp.minimum(block + 1, count - 1)
            values = piece[block, :, HD:]
            for span in range(spans):
                held[1 - slot, span] = score(piece, span, following)
                scores = held[slot, span]
                seen = key_places[number * count + block] <= query_places[span]
                old = peak[span]
                top = jnp.max(scores, axis=1, keepdims=True)
                new = jnp.where(seen, jnp.maximum(old, top), old)
                guard = jnp.where(seen, new, 1e30)
                wide = jnp.concatenate([guard] * (width // HD), axis=1)
                expo = jnp.exp2((scores - wide) * factor)
                shrink = jnp.exp2((old - new) * factor)
                part = expo[:, :HD]
                for lane in range(HD, width, HD):
                    part = part + expo[:, lane : lane + HD]
                peak[span] = new
                total[span] = total[span] * shrink + part
                accum[span] = accum[span] * shrink + jnp.dot(
                    expo.astype(jnp.bfloat16), values, preferred_element_type=jnp.float32
                )

    for number, piece in enumerate(pieces):
        for span in range(spans):
            held[0, span] = score(piece, span, 0)

        def step(pair, carry, number=number, piece=piece):
            two_blocks(number, piece, pair)
            return carry

        lax.fori_loop(0, count // 2, step, 0)
    if last:
        for span in range(spans):
            whole = jnp.sum(total[span], axis=1, keepdims=True)
            out[span] = (accum[span] / whole).astype(jnp.bfloat16)


def attend(key_places, query_places, query, pieces, state, last=False):
    spans, rows, _ = query.shape
    count, width, _ = pieces[0].shape
    wide = jax.ShapeDtypeStruct((spans, rows, HD), jnp.float32)
    smem = pl.BlockSpec(memory_space=pltpu.SMEM)
    vmem = pl.BlockSpec(memory_space=pltpu.VMEM)
    scratch = [pltpu.VMEM((spans, rows, HD), jnp.float32)] * 3 if last else []
    return pl.pallas_call(
        functools.partial(attend_kernel, len(pieces), last, state is None),
        out_shape=jax.ShapeDtypeStruct((spans, rows, HD), jnp.bfloat16) if last else (wide,) * 3,
        in_specs=[smem, smem, vmem] + [vmem] * (len(pieces) + (0 if state is None else 3)),
        out_specs=vmem if last else (vmem,) * 3,
        scratch_shapes=scratch + [pltpu.VMEM((2, spans, rows, width), jnp.float32)],
        compiler_params=pltpu.CompilerParams(vmem_limit_bytes=24 * 1024 * 1024),
        cost_estimate=pl.CostEstimate(flops=1000, bytes_accessed=1000, transcendentals=0),
    )(key_places, query_places, query, *pieces, *(() if state is None else state))


def body(latents, span_order, modulation, qkv_weight, out_weight, up_weight, down_weight):
    place = lax.axis_index("span")
    core, xh, y = place % 2, place // 2 % 2, place // 4
    rows = latents.astype(jnp.float32).transpose(1, 0, 2)
    gate1, shift2, scale2, gate2 = (modulation[:, None, i] for i in range(2, 6))

    depth = qkv_weight.shape[1] // 2
    qkv_mine = send(lax.dynamic_slice_in_dim(qkv_weight, core * depth, depth, 1), x_lane)
    qkv_mine, out_from = hold((qkv_mine, out_weight))
    qkv_rest = send(qkv_mine, other_core)
    out_other = send(out_from, x_lane)
    normed = gather_z(norm_rows(latents, modulation))
    normed = [jnp.concatenate(normed[:5], 1), jnp.concatenate(normed[5:], 1)]
    qkv_other = jnp.concatenate(
        [jnp.where(core == 0, qkv_mine, qkv_rest), jnp.where(core == 0, qkv_rest, qkv_mine)], 1
    )

    qkv_other, out_other = hold((qkv_other, out_other))

    def project(weight):
        parts = [
            jnp.einsum("jtd,sdf->sjtf", tokens, weight, preferred_element_type=jnp.float32)
            for tokens in normed
        ]
        return jnp.concatenate([part.astype(jnp.bfloat16) for part in parts], 2)

    query1, key1, value1 = project(qkv_other)
    got_pair = send(jnp.concatenate([key1, value1, query1], -1), x_pair)
    got_cross = send(jnp.concatenate([key1, value1], -1), x_cross)
    query0, key0, value0 = project(qkv_weight)
    both0 = jnp.concatenate([key0, value0], -1)
    got_two = send(both0, x_two)
    query = jnp.concatenate([query0, got_pair[..., 2 * HD :]], 1)
    piece = jnp.concatenate(
        [
            jnp.concatenate([both0, got_pair[..., : 2 * HD]], 1),
            jnp.concatenate([got_two, got_cross], 1),
        ],
        0,
    )
    half = up_weight.shape[1] // 2
    def places(at_y, at_core):
        own = 2 * (4 * (at_y % Y) + 2 * xh + at_core)
        far = 2 * (4 * (at_y % Y) + 2 * (1 - xh) + at_core)
        return jnp.concatenate(
            [lax.dynamic_slice_in_dim(span_order, own, 2), lax.dynamic_slice_in_dim(span_order, far, 2)]
        )

    mine = lax.dynamic_slice_in_dim(span_order, 2 * place, 2)
    pair_y, cross_y = y + 1 - 2 * (y % 2), y - 1 + 2 * (y % 2) + Y
    near_y = jnp.where(core == 0, pair_y, cross_y)
    next_y = jnp.where(core == 0, cross_y, pair_y)
    here_at, first_at, second_at, far_at, rest_at, mine, piece = hold(
        (
            jnp.concatenate([places(y, core), places(y, 1 - core)]),
            jnp.concatenate([places(near_y, core), places(next_y, 1 - core)]),
            jnp.concatenate([places(near_y, 1 - core), places(next_y, core)]),
            places(y + 2, core),
            places(y + 2, 1 - core),
            mine,
            piece,
        )
    )
    near = send(piece, y_lane)
    beside = send(piece, other_core)
    near_beside = send(beside, y_lane)
    up_from, _ = hold((up_weight, beside))
    up_mine = send(lax.dynamic_slice_in_dim(up_from, core * half, half, 1), x_lane)
    state = attend(here_at, mine, query, [piece, beside], None)
    near, near_beside, state = hold((near, near_beside, state))
    far = send(near, y_lane_back)
    near_rest, beside_rest = send(near, other_core), send(near_beside, other_core)
    state = attend(first_at, mine, query, [near, near_rest], state)
    state = attend(second_at, mine, query, [near_beside, beside_rest], state)
    far, state, up_mine, down_from = hold((far, state, up_mine, down_weight))
    quarter = half // 2
    down_first = lax.dynamic_slice_in_dim(down_from, core * half, quarter, 0)
    down_first = send(down_first, x_lane)
    far_rest = send(far, other_core)
    state = attend(far_at, mine, query, [far], state)
    attended = attend(rest_at, mine, query, [far_rest], state, True)
    tokens = attended.shape[1] // 2
    attended = jnp.concatenate([attended[:, :tokens], send(attended[:, tokens:], x_pair)], -1)
    part = jnp.einsum(
        "jtk,kd->jtd",
        attended,
        jnp.concatenate([out_weight, out_other], 0),
        preferred_element_type=jnp.float32,
    ).astype(jnp.bfloat16)
    up_rest = send(up_mine, other_core)
    part, down_first, down_from = hold((part, down_first, down_from))
    down_second = lax.dynamic_slice_in_dim(down_from, core * half + quarter, quarter, 0)
    down_second = send(down_second, x_lane)
    attn_sum, down_second = scatter_sum_z(jnp.split(part, Z, 1), down_second)
    down_mine = jnp.concatenate([down_first, down_second], 0)
    down_rest = send(down_mine, other_core)
    residual = (rows + gate1 * attn_sum).astype(jnp.bfloat16)
    second = norm_mod(residual.astype(jnp.float32), shift2, scale2)
    second = gather_z(second)

    def feed(blocks):
        tokens = jnp.concatenate(blocks, 1)
        part = None
        for up, down in ((up_weight, down_weight), (up_mine, down_mine), (up_rest, down_rest)):
            hidden = jax.nn.gelu(
                jnp.einsum("jtd,df->jtf", tokens, up, preferred_element_type=jnp.float32),
                approximate=True,
            ).astype(jnp.bfloat16)
            more = jnp.einsum("jtf,fd->jtd", hold(hidden), down, preferred_element_type=jnp.float32)
            part = more if part is None else part + more
        part = part.astype(jnp.bfloat16)
        return jnp.split(part, len(blocks), 1)

    ffn_sum = scatter_sum_z(feed(second[:5]) + feed(second[5:]))
    mixed = residual.astype(jnp.float32) + gate2 * ffn_sum
    return mixed.astype(jnp.bfloat16).transpose(1, 0, 2)


def solution(mesh):
    return jax.shard_map(
        body,
        mesh=mesh,
        in_specs=(
            P("space", "span", None),
            P(),
            P("span", None, None),
            P(None, None, "space"),
            P("space", None),
            P(None, "space"),
            P("space", None),
        ),
        out_specs=P("space", "span", None),
        check_vma=False,
    )
```

```python
import functools

import jax
import jax.numpy as jnp
from jax import lax
from jax.experimental import pallas as pl
from jax.experimental.pallas import tpu as pltpu
from jax.sharding import PartitionSpec as P

HD = 128
Y, X, CORES, Z = 4, 4, 2, 8
AXES = ("span", "space")


def norm_mod(rows, shift, scale):
    mean = jnp.mean(rows, axis=-1, keepdims=True)
    centred = rows - mean
    variance = jnp.mean(centred * centred, axis=-1, keepdims=True)
    return (centred * lax.rsqrt(variance + 1e-06) * (1.0 + scale) + shift).astype(jnp.bfloat16)


def number(y, x, core, z):
    return (((y % Y) * 2 + (x % X) // 2) * CORES + core) * 16 + (x % X) % 2 * Z + z % Z


def send(value, move):
    pairs = []
    for y in range(Y):
        for x in range(X):
            for core in range(CORES):
                for z in range(Z):
                    pairs.append((number(y, x, core, z), number(*move(y, x, core, z))))
    return lax.ppermute(value, AXES, pairs)


def z_pair(y, x, core, z):
    return y, x, core, z ^ 1


def z_cross(y, x, core, z):
    return y, x, core, (z + 1 if z % 2 else z - 1)


def x_pair(y, x, core, z):
    return y, x ^ 1, core, z


def x_cross(y, x, core, z):
    return y, (x + 1 if x % 2 else x - 1), core, z


def x_two(y, x, core, z):
    return y, x + 2, core, z


def x_lane(y, x, core, z):
    return (x_pair if core == 0 else x_cross)(y, x, core, z)


def other_core(y, x, core, z):
    return y, x, 1 - core, z


def y_pair(y, x, core, z):
    return y ^ 1, x, core, z


def y_cross(y, x, core, z):
    return (y + 1 if y % 2 else y - 1), x, core, z


def y_lane(y, x, core, z):
    return (y_pair if core == 0 else y_cross)(y, x, core, z)


def y_lane_back(y, x, core, z):
    return (y_cross if core == 0 else y_pair)(y, x, core, z)


hold = lax.optimization_barrier


def gather_z(mine):
    chains = []
    for span in range(2):
        near = far = mine[span : span + 1]
        blocks = [near]
        for _ in range(3):
            near, far = send(far, z_pair), send(near, z_cross)
            blocks += [near, far]
        blocks.append(send(far, z_pair) if span == 0 else send(near, z_cross))
        chains.append(blocks)
    return [jnp.concatenate(both, 0) for both in zip(*chains)]


def plus(a, b):
    return (a.astype(jnp.float32) + b.astype(jnp.float32)).astype(jnp.bfloat16)


def scatter_sum_z(blocks, rider=None):
    own, near1, far1, near2, far2, near3, far3, last = blocks
    pair, cross = hold((send(last[:1], z_pair), send(last[1:], z_cross)))
    zero = jnp.bfloat16(0)
    near3 = plus(near3, lax.pad(cross, zero, ((1, 0, 0), (0, 0, 0), (0, 0, 0))))
    far3 = plus(far3, lax.pad(pair, zero, ((0, 1, 0), (0, 0, 0), (0, 0, 0))))
    pair, cross = hold((send(near3, z_pair), send(far3, z_cross)))
    pair, cross = send(plus(near2, cross), z_pair), send(plus(far2, pair), z_cross)
    if rider is None:
        pair, cross = hold((pair, cross))
    else:
        pair, cross, rider = hold((pair, cross, rider))
    pair, cross = send(plus(near1, cross), z_pair), send(plus(far1, pair), z_cross)
    total = own.astype(jnp.float32) + pair.astype(jnp.float32) + cross.astype(jnp.float32)
    return total if rider is None else (total, rider)


def norm_kernel(rows, modulation, out):
    for span in range(out.shape[0]):
        shift, scale = modulation[0, span : span + 1, :], modulation[1, span : span + 1, :]
        out[span] = norm_mod(rows[:, span, :].astype(jnp.float32), shift, scale)


def norm_rows(rows, modulation):
    vmem = pl.BlockSpec(memory_space=pltpu.VMEM)
    tokens, spans, width = rows.shape
    return pl.pallas_call(
        norm_kernel,
        out_shape=jax.ShapeDtypeStruct((spans, tokens, width), jnp.bfloat16),
        in_specs=[vmem, vmem],
        out_specs=vmem,
    )(rows, modulation.transpose(1, 0, 2))


def attend_kernel(n_pieces, last, first, key_places, query_places, query, *rest):
    pieces, rest = rest[:n_pieces], rest[n_pieces:]
    if not first:
        peak_in, total_in, accum_in = rest[:3]
        rest = rest[3:]
    if last:
        out, peak, total, accum, held = rest
    else:
        peak, total, accum, held = rest
    spans = query.shape[0]
    if first:
        peak[...] = jnp.full(peak.shape, -1e30, jnp.float32)
        total[...] = jnp.zeros(total.shape, jnp.float32)
        accum[...] = jnp.zeros(accum.shape, jnp.float32)
    else:
        peak[...] = peak_in[...]
        total[...] = total_in[...]
        accum[...] = accum_in[...]
    factor = 1.4426950408889634 / HD**0.5
    count, width, _ = pieces[0].shape

    def score(piece, span, block):
        return lax.dot_general(
            query[span],
            piece[block, :, :HD],
            (((1,), (1,)), ((), ())),
            preferred_element_type=jnp.float32,
        )

    def two_blocks(number, piece, pair):
        for slot in range(2):
            block = 2 * pair + slot
            following = jnp.minimum(block + 1, count - 1)
            values = piece[block, :, HD:]
            for span in range(spans):
                held[1 - slot, span] = score(piece, span, following)
                scores = held[slot, span]
                seen = key_places[number * count + block] <= query_places[span]
                old = peak[span]
                top = jnp.max(scores, axis=1, keepdims=True)
                new = jnp.where(seen, jnp.maximum(old, top), old)
                guard = jnp.where(seen, new, 1e30)
                wide = jnp.concatenate([guard] * (width // HD), axis=1)
                expo = jnp.exp2((scores - wide) * factor)
                shrink = jnp.exp2((old - new) * factor)
                part = expo[:, :HD]
                for lane in range(HD, width, HD):
                    part = part + expo[:, lane : lane + HD]
                peak[span] = new
                total[span] = total[span] * shrink + part
                accum[span] = accum[span] * shrink + jnp.dot(
                    expo.astype(jnp.bfloat16), values, preferred_element_type=jnp.float32
                )

    for number, piece in enumerate(pieces):
        for span in range(spans):
            held[0, span] = score(piece, span, 0)

        def step(pair, carry, number=number, piece=piece):
            two_blocks(number, piece, pair)
            return carry

        lax.fori_loop(0, count // 2, step, 0)
    if last:
        for span in range(spans):
            whole = jnp.sum(total[span], axis=1, keepdims=True)
            out[span] = (accum[span] / whole).astype(jnp.bfloat16)


def attend(key_places, query_places, query, pieces, state, last=False):
    spans, rows, _ = query.shape
    count, width, _ = pieces[0].shape
    wide = jax.ShapeDtypeStruct((spans, rows, HD), jnp.float32)
    smem = pl.BlockSpec(memory_space=pltpu.SMEM)
    vmem = pl.BlockSpec(memory_space=pltpu.VMEM)
    scratch = [pltpu.VMEM((spans, rows, HD), jnp.float32)] * 3 if last else []
    return pl.pallas_call(
        functools.partial(attend_kernel, len(pieces), last, state is None),
        out_shape=jax.ShapeDtypeStruct((spans, rows, HD), jnp.bfloat16) if last else (wide,) * 3,
        in_specs=[smem, smem, vmem] + [vmem] * (len(pieces) + (0 if state is None else 3)),
        out_specs=vmem if last else (vmem,) * 3,
        scratch_shapes=scratch + [pltpu.VMEM((2, spans, rows, width), jnp.float32)],
        compiler_params=pltpu.CompilerParams(vmem_limit_bytes=24 * 1024 * 1024),
        cost_estimate=pl.CostEstimate(flops=1000, bytes_accessed=1000, transcendentals=0),
    )(key_places, query_places, query, *pieces, *(() if state is None else state))


def body(latents, span_order, modulation, qkv_weight, out_weight, up_weight, down_weight):
    place = lax.axis_index("span")
    core, xh, y = place % 2, place // 2 % 2, place // 4
    rows = latents.astype(jnp.float32).transpose(1, 0, 2)
    gate1, shift2, scale2, gate2 = (modulation[:, None, i] for i in range(2, 6))

    depth = qkv_weight.shape[1] // 2
    qkv_mine = send(lax.dynamic_slice_in_dim(qkv_weight, core * depth, depth, 1), x_lane)
    qkv_rest = send(qkv_mine, other_core)
    normed = gather_z(norm_rows(latents, modulation))
    normed = [jnp.concatenate(normed[:5], 1), jnp.concatenate(normed[5:], 1)]
    qkv_other = jnp.concatenate(
        [jnp.where(core == 0, qkv_mine, qkv_rest), jnp.where(core == 0, qkv_rest, qkv_mine)], 1
    )

    def project(weight):
        parts = [
            jnp.einsum("jtd,sdf->sjtf", tokens, weight, preferred_element_type=jnp.float32)
            for tokens in normed
        ]
        return jnp.concatenate([part.astype(jnp.bfloat16) for part in parts], 2)

    query1, key1, value1 = project(qkv_other)
    got_pair = send(jnp.concatenate([key1, value1, query1], -1), x_pair)
    got_cross = send(jnp.concatenate([key1, value1], -1), x_cross)
    query0, key0, value0 = project(qkv_weight)
    both0 = jnp.concatenate([key0, value0], -1)
    got_two = send(both0, x_two)
    half = up_weight.shape[1] // 2
    up_from, down_from, both0 = hold((up_weight, down_weight, both0))
    up_half = lax.dynamic_slice_in_dim(up_from, core * half, half, 1)
    query = jnp.concatenate([query0, got_pair[..., 2 * HD :]], 1)
    piece = jnp.concatenate(
        [
            jnp.concatenate([both0, got_pair[..., : 2 * HD]], 1),
            jnp.concatenate([got_two, got_cross], 1),
        ],
        0,
    )
    half = up_weight.shape[1] // 2
    def places(at_y, at_core):
        own = 2 * (4 * (at_y % Y) + 2 * xh + at_core)
        far = 2 * (4 * (at_y % Y) + 2 * (1 - xh) + at_core)
        return jnp.concatenate(
            [lax.dynamic_slice_in_dim(span_order, own, 2), lax.dynamic_slice_in_dim(span_order, far, 2)]
        )

    mine = lax.dynamic_slice_in_dim(span_order, 2 * place, 2)
    pair_y, cross_y = y + 1 - 2 * (y % 2), y - 1 + 2 * (y % 2) + Y
    near_y = jnp.where(core == 0, pair_y, cross_y)
    next_y = jnp.where(core == 0, cross_y, pair_y)
    here_at, first_at, second_at, far_at, rest_at, mine, piece = hold(
        (
            jnp.concatenate([places(y, core), places(y, 1 - core)]),
            jnp.concatenate([places(near_y, core), places(next_y, 1 - core)]),
            jnp.concatenate([places(near_y, 1 - core), places(next_y, core)]),
            places(y + 2, core),
            places(y + 2, 1 - core),
            mine,
            piece,
        )
    )
    near = send(piece, y_lane)
    beside = send(piece, other_core)
    near_beside = send(beside, y_lane)
    out_from, up_half, _ = hold((out_weight, up_half, beside))
    out_other = send(out_from, x_lane)
    up_mine = send(up_half, x_lane)
    state = attend(here_at, mine, query, [piece, beside], None)
    near, near_beside, state, out_other = hold((near, near_beside, state, out_other))
    far = send(near, y_lane_back)
    near_rest, beside_rest = send(near, other_core), send(near_beside, other_core)
    state = attend(first_at, mine, query, [near, near_rest], state)
    down_from, _ = hold((down_from, near))
    down_half = lax.dynamic_slice_in_dim(down_from, core * half, half, 0)
    state = attend(second_at, mine, query, [near_beside, beside_rest], state)
    far, state, up_mine, down_half = hold((far, state, up_mine, down_half))
    far_rest = send(far, other_core)
    state = attend(far_at, mine, query, [far], state)
    attended = attend(rest_at, mine, query, [far_rest], state, True)
    tokens = attended.shape[1] // 2
    attended = jnp.concatenate([attended[:, :tokens], send(attended[:, tokens:], x_pair)], -1)
    part = jnp.einsum(
        "jtk,kd->jtd",
        attended,
        jnp.concatenate([out_weight, out_other], 0),
        preferred_element_type=jnp.float32,
    ).astype(jnp.bfloat16)
    up_rest = send(up_mine, other_core)
    part, down_half = hold((part, down_half))
    down_first = send(down_half[: half // 2], x_lane)
    attn_sum, down_first = scatter_sum_z(jnp.split(part, Z, 1), down_first)
    down_half, down_first = hold((down_half, down_first))
    down_second = send(down_half[half // 2 :], x_lane)
    down_mine = jnp.concatenate([down_first, down_second], 0)
    down_rest = send(down_mine, other_core)
    residual = (rows + gate1 * attn_sum).astype(jnp.bfloat16)
    second = norm_mod(residual.astype(jnp.float32), shift2, scale2)
    second = gather_z(second)

    def feed(blocks):
        tokens = jnp.concatenate(blocks, 1)
        part = None
        for up, down in ((up_weight, down_weight), (up_mine, down_mine), (up_rest, down_rest)):
            hidden = jax.nn.gelu(
                jnp.einsum("jtd,df->jtf", tokens, up, preferred_element_type=jnp.float32),
                approximate=True,
            ).astype(jnp.bfloat16)
            more = jnp.einsum("jtf,fd->jtd", hold(hidden), down, preferred_element_type=jnp.float32)
            part = more if part is None else part + more
        part = part.astype(jnp.bfloat16)
        return jnp.split(part, len(blocks), 1)

    ffn_sum = scatter_sum_z(feed(second[:5]) + feed(second[5:]))
    mixed = residual.astype(jnp.float32) + gate2 * ffn_sum
    return mixed.astype(jnp.bfloat16).transpose(1, 0, 2)


def solution(mesh):
    return jax.shard_map(
        body,
        mesh=mesh,
        in_specs=(
            P("space", "span", None),
            P(),
            P("span", None, None),
            P(None, None, "space"),
            P("space", None),
            P(None, "space"),
            P("space", None),
        ),
        out_specs=P("space", "span", None),
        check_vma=False,
    )
```

```python
import functools

import jax
import jax.numpy as jnp
from jax import lax
from jax.experimental import pallas as pl
from jax.experimental.pallas import tpu as pltpu
from jax.sharding import PartitionSpec as P

HD = 128
Y, X, CORES, Z = 4, 4, 2, 8
AXES = ("span", "space")


def norm_mod(rows, shift, scale):
    mean = jnp.mean(rows, axis=-1, keepdims=True)
    centred = rows - mean
    variance = jnp.mean(centred * centred, axis=-1, keepdims=True)
    return (centred * lax.rsqrt(variance + 1e-06) * (1.0 + scale) + shift).astype(jnp.bfloat16)


def number(y, x, core, z):
    return (((y % Y) * 2 + (x % X) // 2) * CORES + core) * 16 + (x % X) % 2 * Z + z % Z


def send(value, move):
    pairs = []
    for y in range(Y):
        for x in range(X):
            for core in range(CORES):
                for z in range(Z):
                    pairs.append((number(y, x, core, z), number(*move(y, x, core, z))))
    return lax.ppermute(value, AXES, pairs)


def z_pair(y, x, core, z):
    return y, x, core, z ^ 1


def z_cross(y, x, core, z):
    return y, x, core, (z + 1 if z % 2 else z - 1)


def x_pair(y, x, core, z):
    return y, x ^ 1, core, z


def x_cross(y, x, core, z):
    return y, (x + 1 if x % 2 else x - 1), core, z


def x_two(y, x, core, z):
    return y, x + 2, core, z


def x_lane(y, x, core, z):
    return (x_pair if core == 0 else x_cross)(y, x, core, z)


def other_core(y, x, core, z):
    return y, x, 1 - core, z


def y_pair(y, x, core, z):
    return y ^ 1, x, core, z


def y_cross(y, x, core, z):
    return (y + 1 if y % 2 else y - 1), x, core, z


def y_lane(y, x, core, z):
    return (y_pair if core == 0 else y_cross)(y, x, core, z)


def y_lane_back(y, x, core, z):
    return (y_cross if core == 0 else y_pair)(y, x, core, z)


hold = lax.optimization_barrier


def gather_z(mine):
    chains = []
    for span in range(2):
        near = far = mine[span]
        blocks = [near]
        for _ in range(3):
            near, far = send(far, z_pair), send(near, z_cross)
            blocks += [near, far]
        blocks.append(send(far, z_pair) if span == 0 else send(near, z_cross))
        chains.append(blocks)
    return [jnp.concatenate(both, 0) for both in zip(*chains)]


def plus(a, b):
    return (a.astype(jnp.float32) + b.astype(jnp.float32)).astype(jnp.bfloat16)


def scatter_sum_z(blocks, rider=None):
    own, near1, far1, near2, far2, near3, far3, last = blocks
    pair, cross = hold((send(last[:1], z_pair), send(last[1:], z_cross)))
    zero = jnp.bfloat16(0)
    near3 = plus(near3, lax.pad(cross, zero, ((1, 0, 0), (0, 0, 0), (0, 0, 0))))
    far3 = plus(far3, lax.pad(pair, zero, ((0, 1, 0), (0, 0, 0), (0, 0, 0))))
    pair, cross = hold((send(near3, z_pair), send(far3, z_cross)))
    pair, cross = send(plus(near2, cross), z_pair), send(plus(far2, pair), z_cross)
    if rider is None:
        pair, cross = hold((pair, cross))
    else:
        pair, cross, rider = hold((pair, cross, rider))
    pair, cross = send(plus(near1, cross), z_pair), send(plus(far1, pair), z_cross)
    total = own.astype(jnp.float32) + pair.astype(jnp.float32) + cross.astype(jnp.float32)
    return total if rider is None else (total, rider)


def norm_kernel(rows, modulation, *outs):
    for span, out in enumerate(outs):
        shift, scale = modulation[0, span : span + 1, :], modulation[1, span : span + 1, :]
        out[0] = norm_mod(rows[:, span, :].astype(jnp.float32), shift, scale)


def norm_rows(rows, modulation):
    vmem = pl.BlockSpec(memory_space=pltpu.VMEM)
    tokens, spans, width = rows.shape
    return pl.pallas_call(
        norm_kernel,
        out_shape=(jax.ShapeDtypeStruct((1, tokens, width), jnp.bfloat16),) * spans,
        in_specs=[vmem, vmem],
        out_specs=(vmem,) * spans,
    )(rows, modulation.transpose(1, 0, 2))


def attend_kernel(n_pieces, last, first, key_places, query_places, query, *rest):
    pieces, rest = rest[:n_pieces], rest[n_pieces:]
    if not first:
        peak_in, total_in, accum_in = rest[:3]
        rest = rest[3:]
    if last:
        out, peak, total, accum, held = rest
    else:
        peak, total, accum, held = rest
    spans = query.shape[0]
    if first:
        peak[...] = jnp.full(peak.shape, -1e30, jnp.float32)
        total[...] = jnp.zeros(total.shape, jnp.float32)
        accum[...] = jnp.zeros(accum.shape, jnp.float32)
    else:
        peak[...] = peak_in[...]
        total[...] = total_in[...]
        accum[...] = accum_in[...]
    factor = 1.4426950408889634 / HD**0.5
    count, width, _ = pieces[0].shape

    def score(piece, span, block):
        return lax.dot_general(
            query[span],
            piece[block, :, :HD],
            (((1,), (1,)), ((), ())),
            preferred_element_type=jnp.float32,
        )

    def two_blocks(number, piece, pair):
        for slot in range(2):
            block = 2 * pair + slot
            following = jnp.minimum(block + 1, count - 1)
            values = piece[block, :, HD:]
            for span in range(spans):
                held[1 - slot, span] = score(piece, span, following)
                scores = held[slot, span]
                seen = key_places[number * count + block] <= query_places[span]
                old = peak[span]
                top = jnp.max(scores, axis=1, keepdims=True)
                new = jnp.where(seen, jnp.maximum(old, top), old)
                guard = jnp.where(seen, new, 1e30)
                wide = jnp.concatenate([guard] * (width // HD), axis=1)
                expo = jnp.exp2((scores - wide) * factor)
                shrink = jnp.exp2((old - new) * factor)
                part = expo[:, :HD]
                for lane in range(HD, width, HD):
                    part = part + expo[:, lane : lane + HD]
                peak[span] = new
                total[span] = total[span] * shrink + part
                accum[span] = accum[span] * shrink + jnp.dot(
                    expo.astype(jnp.bfloat16), values, preferred_element_type=jnp.float32
                )

    for number, piece in enumerate(pieces):
        for span in range(spans):
            held[0, span] = score(piece, span, 0)

        def step(pair, carry, number=number, piece=piece):
            two_blocks(number, piece, pair)
            return carry

        lax.fori_loop(0, count // 2, step, 0)
    if last:
        for span in range(spans):
            whole = jnp.sum(total[span], axis=1, keepdims=True)
            out[span] = (accum[span] / whole).astype(jnp.bfloat16)


def attend(key_places, query_places, query, pieces, state, last=False):
    spans, rows, _ = query.shape
    count, width, _ = pieces[0].shape
    wide = jax.ShapeDtypeStruct((spans, rows, HD), jnp.float32)
    smem = pl.BlockSpec(memory_space=pltpu.SMEM)
    vmem = pl.BlockSpec(memory_space=pltpu.VMEM)
    scratch = [pltpu.VMEM((spans, rows, HD), jnp.float32)] * 3 if last else []
    return pl.pallas_call(
        functools.partial(attend_kernel, len(pieces), last, state is None),
        out_shape=jax.ShapeDtypeStruct((spans, rows, HD), jnp.bfloat16) if last else (wide,) * 3,
        in_specs=[smem, smem, vmem] + [vmem] * (len(pieces) + (0 if state is None else 3)),
        out_specs=vmem if last else (vmem,) * 3,
        scratch_shapes=scratch + [pltpu.VMEM((2, spans, rows, width), jnp.float32)],
        compiler_params=pltpu.CompilerParams(vmem_limit_bytes=24 * 1024 * 1024),
        cost_estimate=pl.CostEstimate(flops=1000, bytes_accessed=1000, transcendentals=0),
    )(key_places, query_places, query, *pieces, *(() if state is None else state))


def body(latents, span_order, modulation, qkv_weight, out_weight, up_weight, down_weight):
    place = lax.axis_index("span")
    core, xh, y = place % 2, place // 2 % 2, place // 4
    rows = latents.astype(jnp.float32).transpose(1, 0, 2)
    gate1, shift2, scale2, gate2 = (modulation[:, None, i] for i in range(2, 6))

    depth = qkv_weight.shape[1] // 2
    qkv_mine = send(lax.dynamic_slice_in_dim(qkv_weight, core * depth, depth, 1), x_lane)
    qkv_rest = send(qkv_mine, other_core)
    qkv_other = jnp.concatenate(
        [jnp.where(core == 0, qkv_mine, qkv_rest), jnp.where(core == 0, qkv_rest, qkv_mine)], 1
    )
    normed = gather_z(norm_rows(latents, modulation))
    normed = [jnp.concatenate(normed[:5], 1), jnp.concatenate(normed[5:], 1)]

    def project(weight):
        parts = [
            jnp.einsum("jtd,sdf->sjtf", tokens, weight, preferred_element_type=jnp.float32)
            for tokens in normed
        ]
        return jnp.concatenate([part.astype(jnp.bfloat16) for part in parts], 2)

    query1, key1, value1 = project(qkv_other)
    got_pair = send(jnp.concatenate([key1, value1, query1], -1), x_pair)
    got_cross = send(jnp.concatenate([key1, value1], -1), x_cross)
    query0, key0, value0 = project(qkv_weight)
    both0 = jnp.concatenate([key0, value0], -1)
    got_two = send(both0, x_two)
    half = up_weight.shape[1] // 2
    up_from, both0 = hold((up_weight, both0))
    up_half = lax.dynamic_slice_in_dim(up_from, core * half, half, 1)
    query = jnp.concatenate([query0, got_pair[..., 2 * HD :]], 1)
    piece = jnp.concatenate(
        [
            jnp.concatenate([both0, got_pair[..., : 2 * HD]], 1),
            jnp.concatenate([got_two, got_cross], 1),
        ],
        0,
    )
    half = up_weight.shape[1] // 2
    def places(at_y, at_core):
        own = 2 * (4 * (at_y % Y) + 2 * xh + at_core)
        far = 2 * (4 * (at_y % Y) + 2 * (1 - xh) + at_core)
        return jnp.concatenate(
            [lax.dynamic_slice_in_dim(span_order, own, 2), lax.dynamic_slice_in_dim(span_order, far, 2)]
        )

    mine = lax.dynamic_slice_in_dim(span_order, 2 * place, 2)
    pair_y, cross_y = y + 1 - 2 * (y % 2), y - 1 + 2 * (y % 2) + Y
    near_y = jnp.where(core == 0, pair_y, cross_y)
    next_y = jnp.where(core == 0, cross_y, pair_y)
    here_at, first_at, second_at, far_at, rest_at, mine, piece = hold(
        (
            jnp.concatenate([places(y, core), places(y, 1 - core)]),
            places(near_y, core),
            jnp.concatenate(
                [places(near_y, 1 - core), places(next_y, 1 - core), places(next_y, core)]
            ),
            places(y + 2, core),
            places(y + 2, 1 - core),
            mine,
            piece,
        )
    )
    near = send(piece, y_lane)
    beside = send(piece, other_core)
    near_beside = send(beside, y_lane)
    out_from, up_half, _ = hold((out_weight, up_half, beside))
    out_other = send(out_from, x_lane)
    up_first = send(up_half[:depth], x_lane)
    state = attend(here_at, mine, query, [piece, beside], None)
    near, state = hold((near, state))
    state = attend(first_at, mine, query, [near], state)
    near_beside, near, state, out_other, up_first, up_half = hold(
        (near_beside, near, state, out_other, up_first, up_half)
    )
    up_second = send(up_half[depth:], x_lane)
    far = send(near, y_lane_back)
    near_rest, beside_rest = send(near, other_core), send(near_beside, other_core)
    state = attend(second_at, mine, query, [near_beside, near_rest, beside_rest], state)
    far, state = hold((far, state))
    far_rest = send(far, other_core)
    state = attend(far_at, mine, query, [far], state)
    attended = attend(rest_at, mine, query, [far_rest], state, True)
    tokens = attended.shape[1] // 2
    down_from, attended, up_second = hold((down_weight, attended, up_second))
    up_mine = jnp.concatenate([up_first, up_second], 0)
    down_half = lax.dynamic_slice_in_dim(down_from, core * half, half, 0)
    attended = jnp.concatenate([attended[:, :tokens], send(attended[:, tokens:], x_pair)], -1)
    part = jnp.einsum(
        "jtk,kd->jtd",
        attended,
        jnp.concatenate([out_weight, out_other], 0),
        preferred_element_type=jnp.float32,
    ).astype(jnp.bfloat16)
    up_rest = send(up_mine, other_core)
    part, down_half = hold((part, down_half))
    down_first = send(down_half[: half // 2], x_lane)
    attn_sum, down_first = scatter_sum_z(jnp.split(part, Z, 1), down_first)
    down_half, down_first = hold((down_half, down_first))
    down_second = send(down_half[half // 2 :], x_lane)
    down_mine = jnp.concatenate([down_first, down_second], 0)
    down_rest = send(down_mine, other_core)
    residual = (rows + gate1 * attn_sum).astype(jnp.bfloat16)
    second = norm_mod(residual.astype(jnp.float32), shift2, scale2)
    second = gather_z((second[:1], second[1:]))

    def feed(blocks):
        tokens = jnp.concatenate(blocks, 1)
        part = None
        for up, down in ((up_weight, down_weight), (up_mine, down_mine), (up_rest, down_rest)):
            hidden = jax.nn.gelu(
                jnp.einsum("jtd,df->jtf", tokens, up, preferred_element_type=jnp.float32),
                approximate=True,
            ).astype(jnp.bfloat16)
            more = jnp.einsum("jtf,fd->jtd", hold(hidden), down, preferred_element_type=jnp.float32)
            part = more if part is None else part + more
        part = part.astype(jnp.bfloat16)
        return jnp.split(part, len(blocks), 1)

    ffn_sum = scatter_sum_z(feed(second[:5]) + feed(second[5:]))
    mixed = residual.astype(jnp.float32) + gate2 * ffn_sum
    return mixed.astype(jnp.bfloat16).transpose(1, 0, 2)


def solution(mesh):
    return jax.shard_map(
        body,
        mesh=mesh,
        in_specs=(
            P("space", "span", None),
            P(),
            P("span", None, None),
            P(None, None, "space"),
            P("space", None),
            P(None, "space"),
            P("space", None),
        ),
        out_specs=P("space", "span", None),
        check_vma=False,
    )
```

```python
import functools

import jax
import jax.numpy as jnp
from jax import lax
from jax.experimental import pallas as pl
from jax.experimental.pallas import tpu as pltpu
from jax.sharding import PartitionSpec as P

HD = 128
Y, X, CORES, Z = 4, 4, 2, 8
AXES = ("span", "space")


def norm_mod(rows, shift, scale):
    mean = jnp.mean(rows, axis=-1, keepdims=True)
    centred = rows - mean
    variance = jnp.mean(centred * centred, axis=-1, keepdims=True)
    return (centred * lax.rsqrt(variance + 1e-06) * (1.0 + scale) + shift).astype(jnp.bfloat16)


def number(y, x, core, z):
    return (((y % Y) * 2 + (x % X) // 2) * CORES + core) * 16 + (x % X) % 2 * Z + z % Z


def send(value, move):
    pairs = []
    for y in range(Y):
        for x in range(X):
            for core in range(CORES):
                for z in range(Z):
                    pairs.append((number(y, x, core, z), number(*move(y, x, core, z))))
    return lax.ppermute(value, AXES, pairs)


def z_pair(y, x, core, z):
    return y, x, core, z ^ 1


def z_cross(y, x, core, z):
    return y, x, core, (z + 1 if z % 2 else z - 1)


def x_pair(y, x, core, z):
    return y, x ^ 1, core, z


def x_cross(y, x, core, z):
    return y, (x + 1 if x % 2 else x - 1), core, z


def x_two(y, x, core, z):
    return y, x + 2, core, z


def x_lane(y, x, core, z):
    return (x_pair if core == 0 else x_cross)(y, x, core, z)


def other_core(y, x, core, z):
    return y, x, 1 - core, z


def y_pair(y, x, core, z):
    return y ^ 1, x, core, z


def y_cross(y, x, core, z):
    return (y + 1 if y % 2 else y - 1), x, core, z


def y_lane(y, x, core, z):
    return (y_pair if core == 0 else y_cross)(y, x, core, z)


def y_lane_back(y, x, core, z):
    return (y_cross if core == 0 else y_pair)(y, x, core, z)


hold = lax.optimization_barrier


def gather_z(mine):
    chains = []
    for span in range(2):
        near = far = mine[span]
        blocks = [near]
        for _ in range(3):
            near, far = send(far, z_pair), send(near, z_cross)
            blocks += [near, far]
        blocks.append(send(far, z_pair) if span == 0 else send(near, z_cross))
        chains.append(blocks)
    return [jnp.concatenate(both, 0) for both in zip(*chains)]


def plus(a, b):
    return (a.astype(jnp.float32) + b.astype(jnp.float32)).astype(jnp.bfloat16)


def scatter_sum_z(blocks, rider=None):
    own, near1, far1, near2, far2, near3, far3, last = blocks
    pair, cross = hold((send(last[:1], z_pair), send(last[1:], z_cross)))
    zero = jnp.bfloat16(0)
    near3 = plus(near3, lax.pad(cross, zero, ((1, 0, 0), (0, 0, 0), (0, 0, 0))))
    far3 = plus(far3, lax.pad(pair, zero, ((0, 1, 0), (0, 0, 0), (0, 0, 0))))
    pair, cross = hold((send(near3, z_pair), send(far3, z_cross)))
    pair, cross = send(plus(near2, cross), z_pair), send(plus(far2, pair), z_cross)
    if rider is None:
        pair, cross = hold((pair, cross))
    else:
        pair, cross, rider = hold((pair, cross, rider))
    pair, cross = send(plus(near1, cross), z_pair), send(plus(far1, pair), z_cross)
    total = own.astype(jnp.float32) + pair.astype(jnp.float32) + cross.astype(jnp.float32)
    return total if rider is None else (total, rider)


def norm_kernel(rows, modulation, *outs):
    for span, out in enumerate(outs):
        shift, scale = modulation[0, span : span + 1, :], modulation[1, span : span + 1, :]
        out[0] = norm_mod(rows[:, span, :].astype(jnp.float32), shift, scale)


def norm_rows(rows, modulation):
    vmem = pl.BlockSpec(memory_space=pltpu.VMEM)
    tokens, spans, width = rows.shape
    return pl.pallas_call(
        norm_kernel,
        out_shape=(jax.ShapeDtypeStruct((1, tokens, width), jnp.bfloat16),) * spans,
        in_specs=[vmem, vmem],
        out_specs=(vmem,) * spans,
    )(rows, modulation.transpose(1, 0, 2))


def attend_kernel(n_pieces, last, first, key_places, query_places, query, *rest):
    pieces, rest = rest[:n_pieces], rest[n_pieces:]
    if not first:
        peak_in, total_in, accum_in = rest[:3]
        rest = rest[3:]
    if last:
        out, peak, total, accum, held = rest
    else:
        peak, total, accum, held = rest
    spans = query.shape[0]
    if first:
        peak[...] = jnp.full(peak.shape, -1e30, jnp.float32)
        total[...] = jnp.zeros(total.shape, jnp.float32)
        accum[...] = jnp.zeros(accum.shape, jnp.float32)
    else:
        peak[...] = peak_in[...]
        total[...] = total_in[...]
        accum[...] = accum_in[...]
    factor = 1.4426950408889634 / HD**0.5
    count, width, _ = pieces[0].shape

    def score(piece, span, block):
        return lax.dot_general(
            query[span],
            piece[block, :, :HD],
            (((1,), (1,)), ((), ())),
            preferred_element_type=jnp.float32,
        )

    def two_blocks(number, piece, pair):
        for slot in range(2):
            block = 2 * pair + slot
            following = jnp.minimum(block + 1, count - 1)
            values = piece[block, :, HD:]
            for span in range(spans):
                held[1 - slot, span] = score(piece, span, following)
                scores = held[slot, span]
                seen = key_places[number * count + block] <= query_places[span]
                old = peak[span]
                top = jnp.max(scores, axis=1, keepdims=True)
                new = jnp.where(seen, jnp.maximum(old, top), old)
                guard = jnp.where(seen, new, 1e30)
                wide = jnp.concatenate([guard] * (width // HD), axis=1)
                expo = jnp.exp2((scores - wide) * factor)
                shrink = jnp.exp2((old - new) * factor)
                part = expo[:, :HD]
                for lane in range(HD, width, HD):
                    part = part + expo[:, lane : lane + HD]
                peak[span] = new
                total[span] = total[span] * shrink + part
                accum[span] = accum[span] * shrink + jnp.dot(
                    expo.astype(jnp.bfloat16), values, preferred_element_type=jnp.float32
                )

    for number, piece in enumerate(pieces):
        for span in range(spans):
            held[0, span] = score(piece, span, 0)

        def step(pair, carry, number=number, piece=piece):
            two_blocks(number, piece, pair)
            return carry

        lax.fori_loop(0, count // 2, step, 0)
    if last:
        for span in range(spans):
            whole = jnp.sum(total[span], axis=1, keepdims=True)
            out[span] = (accum[span] / whole).astype(jnp.bfloat16)


def attend(key_places, query_places, query, pieces, state, last=False):
    spans, rows, _ = query.shape
    count, width, _ = pieces[0].shape
    wide = jax.ShapeDtypeStruct((spans, rows, HD), jnp.float32)
    smem = pl.BlockSpec(memory_space=pltpu.SMEM)
    vmem = pl.BlockSpec(memory_space=pltpu.VMEM)
    scratch = [pltpu.VMEM((spans, rows, HD), jnp.float32)] * 3 if last else []
    return pl.pallas_call(
        functools.partial(attend_kernel, len(pieces), last, state is None),
        out_shape=jax.ShapeDtypeStruct((spans, rows, HD), jnp.bfloat16) if last else (wide,) * 3,
        in_specs=[smem, smem, vmem] + [vmem] * (len(pieces) + (0 if state is None else 3)),
        out_specs=vmem if last else (vmem,) * 3,
        scratch_shapes=scratch + [pltpu.VMEM((2, spans, rows, width), jnp.float32)],
        compiler_params=pltpu.CompilerParams(vmem_limit_bytes=24 * 1024 * 1024),
        cost_estimate=pl.CostEstimate(flops=1000, bytes_accessed=1000, transcendentals=0),
    )(key_places, query_places, query, *pieces, *(() if state is None else state))


def body(latents, span_order, modulation, qkv_weight, out_weight, up_weight, down_weight):
    place = lax.axis_index("span")
    core, xh, y = place % 2, place // 2 % 2, place // 4
    rows = latents.astype(jnp.float32).transpose(1, 0, 2)
    gate1, shift2, scale2, gate2 = (modulation[:, None, i] for i in range(2, 6))

    depth = qkv_weight.shape[1] // 2
    qkv_mine = send(lax.dynamic_slice_in_dim(qkv_weight, core * depth, depth, 1), x_lane)
    qkv_rest = send(qkv_mine, other_core)
    qkv_other = jnp.concatenate(
        [jnp.where(core == 0, qkv_mine, qkv_rest), jnp.where(core == 0, qkv_rest, qkv_mine)], 1
    )
    normed = gather_z(norm_rows(latents, modulation))
    normed = [jnp.concatenate(normed[:5], 1), jnp.concatenate(normed[5:], 1)]

    def project(weight):
        parts = [
            jnp.einsum("jtd,sdf->sjtf", tokens, weight, preferred_element_type=jnp.float32)
            for tokens in normed
        ]
        return jnp.concatenate([part.astype(jnp.bfloat16) for part in parts], 2)

    query1, key1, value1 = project(qkv_other)
    got_pair = send(jnp.concatenate([key1, value1, query1], -1), x_pair)
    got_cross = send(jnp.concatenate([key1, value1], -1), x_cross)
    query0, key0, value0 = project(qkv_weight)
    both0 = jnp.concatenate([key0, value0], -1)
    got_two = send(both0, x_two)
    half = up_weight.shape[1] // 2
    up_from, both0 = hold((up_weight, both0))
    up_half = lax.dynamic_slice_in_dim(up_from, core * half, half, 1)
    got_pair, up_half = hold((got_pair, up_half))
    query = jnp.concatenate([query0, got_pair[..., 2 * HD :]], 1)
    piece = jnp.concatenate(
        [
            jnp.concatenate([both0, got_pair[..., : 2 * HD]], 1),
            jnp.concatenate([got_two, got_cross], 1),
        ],
        0,
    )
    half = up_weight.shape[1] // 2
    def places(at_y, at_core):
        own = 2 * (4 * (at_y % Y) + 2 * xh + at_core)
        far = 2 * (4 * (at_y % Y) + 2 * (1 - xh) + at_core)
        return jnp.concatenate(
            [lax.dynamic_slice_in_dim(span_order, own, 2), lax.dynamic_slice_in_dim(span_order, far, 2)]
        )

    mine = lax.dynamic_slice_in_dim(span_order, 2 * place, 2)
    pair_y, cross_y = y + 1 - 2 * (y % 2), y - 1 + 2 * (y % 2) + Y
    near_y = jnp.where(core == 0, pair_y, cross_y)
    next_y = jnp.where(core == 0, cross_y, pair_y)
    here_at, first_at, second_at, far_at, rest_at, mine, piece = hold(
        (
            jnp.concatenate([places(y, core), places(y, 1 - core)]),
            places(near_y, core),
            jnp.concatenate(
                [places(near_y, 1 - core), places(next_y, 1 - core), places(next_y, core)]
            ),
            places(y + 2, core),
            places(y + 2, 1 - core),
            mine,
            piece,
        )
    )
    near = send(piece, y_lane)
    beside = send(piece, other_core)
    near_beside = send(beside, y_lane)
    out_half = out_weight.shape[0] // 2
    out_from, up_half, _ = hold((out_weight, up_half, beside))
    out_mine = send(lax.dynamic_slice_in_dim(out_from, core * out_half, out_half, 0), x_lane)
    up_first = send(up_half[:depth], x_lane)
    state = attend(here_at, mine, query, [piece, beside], None)
    near, state = hold((near, state))
    state = attend(first_at, mine, query, [near], state)
    near_beside, near, state, out_mine, up_first, up_half = hold(
        (near_beside, near, state, out_mine, up_first, up_half)
    )
    up_second = send(up_half[depth:], x_lane)
    far = send(near, y_lane_back)
    near_rest, beside_rest = send(near, other_core), send(near_beside, other_core)
    state = attend(second_at, mine, query, [near_beside, near_rest, beside_rest], state)
    far, state, out_mine = hold((far, state, out_mine))
    out_rest = send(out_mine, other_core)
    out_other = jnp.concatenate(
        [jnp.where(core == 0, out_mine, out_rest), jnp.where(core == 0, out_rest, out_mine)], 0
    )
    far_rest = send(far, other_core)
    state = attend(far_at, mine, query, [far], state)
    attended = attend(rest_at, mine, query, [far_rest], state, True)
    tokens = attended.shape[1] // 2
    down_from, attended, up_second = hold((down_weight, attended, up_second))
    up_mine = jnp.concatenate([up_first, up_second], 0)
    down_half = lax.dynamic_slice_in_dim(down_from, core * half, half, 0)
    attended = jnp.concatenate([attended[:, :tokens], send(attended[:, tokens:], x_pair)], -1)
    part = jnp.einsum(
        "jtk,kd->jtd",
        attended,
        jnp.concatenate([out_weight, out_other], 0),
        preferred_element_type=jnp.float32,
    ).astype(jnp.bfloat16)
    up_rest = send(up_mine, other_core)
    part, down_half = hold((part, down_half))
    down_first = send(down_half[: half // 2], x_lane)
    attn_sum, down_first = scatter_sum_z(jnp.split(part, Z, 1), down_first)
    down_half, down_first = hold((down_half, down_first))
    down_second = send(down_half[half // 2 :], x_lane)
    down_mine = jnp.concatenate([down_first, down_second], 0)
    down_rest = send(down_mine, other_core)
    residual = (rows + gate1 * attn_sum).astype(jnp.bfloat16)
    second = norm_mod(residual.astype(jnp.float32), shift2, scale2)
    second = gather_z((second[:1], second[1:]))

    def feed(blocks):
        tokens = jnp.concatenate(blocks, 1)
        part = None
        for up, down in ((up_weight, down_weight), (up_mine, down_mine), (up_rest, down_rest)):
            hidden = jax.nn.gelu(
                jnp.einsum("jtd,df->jtf", tokens, up, preferred_element_type=jnp.float32),
                approximate=True,
            ).astype(jnp.bfloat16)
            more = jnp.einsum("jtf,fd->jtd", hold(hidden), down, preferred_element_type=jnp.float32)
            part = more if part is None else part + more
        part = part.astype(jnp.bfloat16)
        return jnp.split(part, len(blocks), 1)

    ffn_sum = scatter_sum_z(feed(second[:5]) + feed(second[5:]))
    mixed = residual.astype(jnp.float32) + gate2 * ffn_sum
    return mixed.astype(jnp.bfloat16).transpose(1, 0, 2)


def solution(mesh):
    return jax.shard_map(
        body,
        mesh=mesh,
        in_specs=(
            P("space", "span", None),
            P(),
            P("span", None, None),
            P(None, None, "space"),
            P("space", None),
            P(None, "space"),
            P("space", None),
        ),
        out_specs=P("space", "span", None),
        check_vma=False,
    )
```

```python
import functools

import jax
import jax.numpy as jnp
from jax import lax
from jax.experimental import pallas as pl
from jax.experimental.pallas import tpu as pltpu
from jax.sharding import PartitionSpec as P

HD = 128
Y, X, CORES, Z = 4, 4, 2, 8
AXES = ("span", "space")


def norm_mod(rows, shift, scale):
    mean = jnp.mean(rows, axis=-1, keepdims=True)
    centred = rows - mean
    variance = jnp.mean(centred * centred, axis=-1, keepdims=True)
    return (centred * lax.rsqrt(variance + 1e-06) * (1.0 + scale) + shift).astype(jnp.bfloat16)


def number(y, x, core, z):
    return (((y % Y) * 2 + (x % X) // 2) * CORES + core) * 16 + (x % X) % 2 * Z + z % Z


def send(value, move):
    pairs = []
    for y in range(Y):
        for x in range(X):
            for core in range(CORES):
                for z in range(Z):
                    pairs.append((number(y, x, core, z), number(*move(y, x, core, z))))
    return lax.ppermute(value, AXES, pairs)


def z_pair(y, x, core, z):
    return y, x, core, z ^ 1


def z_cross(y, x, core, z):
    return y, x, core, (z + 1 if z % 2 else z - 1)


def x_pair(y, x, core, z):
    return y, x ^ 1, core, z


def x_cross(y, x, core, z):
    return y, (x + 1 if x % 2 else x - 1), core, z


def x_two(y, x, core, z):
    return y, x + 2, core, z


def x_lane(y, x, core, z):
    return (x_pair if core == 0 else x_cross)(y, x, core, z)


def other_core(y, x, core, z):
    return y, x, 1 - core, z


def y_pair(y, x, core, z):
    return y ^ 1, x, core, z


def y_cross(y, x, core, z):
    return (y + 1 if y % 2 else y - 1), x, core, z


def y_lane(y, x, core, z):
    return (y_pair if core == 0 else y_cross)(y, x, core, z)


def y_lane_back(y, x, core, z):
    return (y_cross if core == 0 else y_pair)(y, x, core, z)


hold = lax.optimization_barrier


def gather_z(mine):
    chains = []
    for span in range(2):
        near = far = mine[span]
        blocks = [near]
        for _ in range(3):
            near, far = send(far, z_pair), send(near, z_cross)
            blocks += [near, far]
        blocks.append(send(far, z_pair) if span == 0 else send(near, z_cross))
        chains.append(blocks)
    return [jnp.concatenate(both, 0) for both in zip(*chains)]


def plus(a, b):
    return (a.astype(jnp.float32) + b.astype(jnp.float32)).astype(jnp.bfloat16)


def scatter_sum_z(blocks, rider=None):
    own, near1, far1, near2, far2, near3, far3, last = blocks
    pair, cross = hold((send(last[:1], z_pair), send(last[1:], z_cross)))
    zero = jnp.bfloat16(0)
    near3 = plus(near3, lax.pad(cross, zero, ((1, 0, 0), (0, 0, 0), (0, 0, 0))))
    far3 = plus(far3, lax.pad(pair, zero, ((0, 1, 0), (0, 0, 0), (0, 0, 0))))
    pair, cross = hold((send(near3, z_pair), send(far3, z_cross)))
    pair, cross = send(plus(near2, cross), z_pair), send(plus(far2, pair), z_cross)
    if rider is None:
        pair, cross = hold((pair, cross))
    else:
        pair, cross, rider = hold((pair, cross, rider))
    pair, cross = send(plus(near1, cross), z_pair), send(plus(far1, pair), z_cross)
    total = own.astype(jnp.float32) + pair.astype(jnp.float32) + cross.astype(jnp.float32)
    return total if rider is None else (total, rider)


def norm_kernel(rows, modulation, *outs):
    for span, out in enumerate(outs):
        shift, scale = modulation[0, span : span + 1, :], modulation[1, span : span + 1, :]
        out[0] = norm_mod(rows[:, span, :].astype(jnp.float32), shift, scale)


def norm_rows(rows, modulation):
    vmem = pl.BlockSpec(memory_space=pltpu.VMEM)
    tokens, spans, width = rows.shape
    return pl.pallas_call(
        norm_kernel,
        out_shape=(jax.ShapeDtypeStruct((1, tokens, width), jnp.bfloat16),) * spans,
        in_specs=[vmem, vmem],
        out_specs=(vmem,) * spans,
    )(rows, modulation.transpose(1, 0, 2))


def attend_kernel(n_pieces, last, first, key_places, query_places, query, *rest):
    pieces, rest = rest[:n_pieces], rest[n_pieces:]
    if not first:
        peak_in, total_in, accum_in = rest[:3]
        rest = rest[3:]
    if last:
        out, peak, total, accum, held = rest
    else:
        peak, total, accum, held = rest
    spans = query.shape[0]
    if first:
        peak[...] = jnp.full(peak.shape, -1e30, jnp.float32)
        total[...] = jnp.zeros(total.shape, jnp.float32)
        accum[...] = jnp.zeros(accum.shape, jnp.float32)
    else:
        peak[...] = peak_in[...]
        total[...] = total_in[...]
        accum[...] = accum_in[...]
    factor = 1.4426950408889634 / HD**0.5
    count, width, _ = pieces[0].shape

    def score(piece, span, block):
        return lax.dot_general(
            query[span],
            piece[block, :, :HD],
            (((1,), (1,)), ((), ())),
            preferred_element_type=jnp.float32,
        )

    def two_blocks(number, piece, pair):
        for slot in range(2):
            block = 2 * pair + slot
            following = jnp.minimum(block + 1, count - 1)
            values = piece[block, :, HD:]
            for span in range(spans):
                held[1 - slot, span] = score(piece, span, following)
                scores = held[slot, span]
                seen = key_places[number * count + block] <= query_places[span]
                old = peak[span]
                top = jnp.max(scores, axis=1, keepdims=True)
                new = jnp.where(seen, jnp.maximum(old, top), old)
                guard = jnp.where(seen, new, 1e30)
                wide = jnp.concatenate([guard] * (width // HD), axis=1)
                expo = jnp.exp2((scores - wide) * factor)
                shrink = jnp.exp2((old - new) * factor)
                part = expo[:, :HD]
                for lane in range(HD, width, HD):
                    part = part + expo[:, lane : lane + HD]
                peak[span] = new
                total[span] = total[span] * shrink + part
                accum[span] = accum[span] * shrink + jnp.dot(
                    expo.astype(jnp.bfloat16), values, preferred_element_type=jnp.float32
                )

    for number, piece in enumerate(pieces):
        for span in range(spans):
            held[0, span] = score(piece, span, 0)

        def step(pair, carry, number=number, piece=piece):
            two_blocks(number, piece, pair)
            return carry

        lax.fori_loop(0, count // 2, step, 0)
    if last:
        for span in range(spans):
            whole = jnp.sum(total[span], axis=1, keepdims=True)
            out[span] = (accum[span] / whole).astype(jnp.bfloat16)


def attend(key_places, query_places, query, pieces, state, last=False):
    spans, rows, _ = query.shape
    count, width, _ = pieces[0].shape
    wide = jax.ShapeDtypeStruct((spans, rows, HD), jnp.float32)
    smem = pl.BlockSpec(memory_space=pltpu.SMEM)
    vmem = pl.BlockSpec(memory_space=pltpu.VMEM)
    scratch = [pltpu.VMEM((spans, rows, HD), jnp.float32)] * 3 if last else []
    return pl.pallas_call(
        functools.partial(attend_kernel, len(pieces), last, state is None),
        out_shape=jax.ShapeDtypeStruct((spans, rows, HD), jnp.bfloat16) if last else (wide,) * 3,
        in_specs=[smem, smem, vmem] + [vmem] * (len(pieces) + (0 if state is None else 3)),
        out_specs=vmem if last else (vmem,) * 3,
        scratch_shapes=scratch + [pltpu.VMEM((2, spans, rows, width), jnp.float32)],
        compiler_params=pltpu.CompilerParams(vmem_limit_bytes=24 * 1024 * 1024),
        cost_estimate=pl.CostEstimate(flops=1000, bytes_accessed=1000, transcendentals=0),
    )(key_places, query_places, query, *pieces, *(() if state is None else state))


def body(latents, span_order, modulation, qkv_weight, out_weight, up_weight, down_weight):
    place = lax.axis_index("span")
    core, xh, y = place % 2, place // 2 % 2, place // 4
    rows = latents.astype(jnp.float32).transpose(1, 0, 2)
    gate1, shift2, scale2, gate2 = (modulation[:, None, i] for i in range(2, 6))

    depth = qkv_weight.shape[1] // 2
    qkv_mine = send(lax.dynamic_slice_in_dim(qkv_weight, core * depth, depth, 1), x_lane)
    qkv_rest = send(qkv_mine, other_core)
    qkv_other = jnp.concatenate(
        [jnp.where(core == 0, qkv_mine, qkv_rest), jnp.where(core == 0, qkv_rest, qkv_mine)], 1
    )
    normed = gather_z(norm_rows(latents, modulation))
    normed = [jnp.concatenate(normed[:5], 1), jnp.concatenate(normed[5:], 1)]

    def project(weight):
        parts = [
            jnp.einsum("jtd,sdf->sjtf", tokens, weight, preferred_element_type=jnp.float32)
            for tokens in normed
        ]
        return jnp.concatenate([part.astype(jnp.bfloat16) for part in parts], 2)

    query1, key1, value1 = project(qkv_other)
    got_pair = send(jnp.concatenate([key1, value1, query1], -1), x_pair)
    got_cross = send(jnp.concatenate([key1, value1], -1), x_cross)
    query0, key0, value0 = project(qkv_weight)
    both0 = jnp.concatenate([key0, value0], -1)
    got_two = send(both0, x_two)
    half = up_weight.shape[1] // 2
    up_from, both0 = hold((up_weight, both0))
    up_half = lax.dynamic_slice_in_dim(up_from, core * half, half, 1)
    got_pair, up_half = hold((got_pair, up_half))
    query = jnp.concatenate([query0, got_pair[..., 2 * HD :]], 1)
    piece = jnp.concatenate(
        [
            jnp.concatenate([both0, got_pair[..., : 2 * HD]], 1),
            jnp.concatenate([got_two, got_cross], 1),
        ],
        0,
    )
    half = up_weight.shape[1] // 2
    def places(at_y, at_core):
        own = 2 * (4 * (at_y % Y) + 2 * xh + at_core)
        far = 2 * (4 * (at_y % Y) + 2 * (1 - xh) + at_core)
        return jnp.concatenate(
            [lax.dynamic_slice_in_dim(span_order, own, 2), lax.dynamic_slice_in_dim(span_order, far, 2)]
        )

    mine = lax.dynamic_slice_in_dim(span_order, 2 * place, 2)
    pair_y, cross_y = y + 1 - 2 * (y % 2), y - 1 + 2 * (y % 2) + Y
    near_y = jnp.where(core == 0, pair_y, cross_y)
    next_y = jnp.where(core == 0, cross_y, pair_y)
    here_at, first_at, second_at, far_at, rest_at, mine, piece = hold(
        (
            jnp.concatenate([places(y, core), places(y, 1 - core)]),
            places(near_y, core),
            jnp.concatenate(
                [places(near_y, 1 - core), places(next_y, 1 - core), places(next_y, core)]
            ),
            places(y + 2, core),
            places(y + 2, 1 - core),
            mine,
            piece,
        )
    )
    near = send(piece, y_lane)
    beside = send(piece, other_core)
    near_beside = send(beside, y_lane)
    out_half = out_weight.shape[0] // 2
    out_from, up_half, _ = hold((out_weight, up_half, beside))
    out_mine = send(lax.dynamic_slice_in_dim(out_from, core * out_half, out_half, 0), x_lane)
    up_first = send(up_half[:depth], x_lane)
    state = attend(here_at, mine, query, [piece, beside], None)
    near, state = hold((near, state))
    state = attend(first_at, mine, query, [near], state)
    near_beside, near, state, out_mine, up_first, up_half = hold(
        (near_beside, near, state, out_mine, up_first, up_half)
    )
    up_second = send(up_half[depth:], x_lane)
    far = send(near, y_lane_back)
    near_rest, beside_rest = send(near, other_core), send(near_beside, other_core)
    state = attend(second_at, mine, query, [near_beside, near_rest, beside_rest], state)
    far, state, out_mine = hold((far, state, out_mine))
    out_rest = send(out_mine, other_core)
    out_other = jnp.concatenate(
        [jnp.where(core == 0, out_mine, out_rest), jnp.where(core == 0, out_rest, out_mine)], 0
    )
    far_rest = send(far, other_core)
    state = attend(far_at, mine, query, [far], state)
    attended = attend(rest_at, mine, query, [far_rest], state, True)
    tokens = attended.shape[1] // 2
    down_from, attended, up_second = hold((down_weight, attended, up_second))
    up_mine = jnp.concatenate([up_first, up_second], 0)
    down_half = lax.dynamic_slice_in_dim(down_from, core * half, half, 0)
    attended = jnp.concatenate([attended[:, :tokens], send(attended[:, tokens:], x_pair)], -1)
    part = jnp.einsum(
        "jtk,kd->jtd",
        attended,
        jnp.concatenate([out_weight, out_other], 0),
        preferred_element_type=jnp.float32,
    ).astype(jnp.bfloat16)
    up_rest = send(up_mine, other_core)
    part, down_half = hold((part, down_half))
    down_first = send(down_half[: half // 2], x_lane)
    attn_sum, down_first = scatter_sum_z(jnp.split(part, Z, 1), down_first)
    down_half, down_first = hold((down_half, down_first))
    down_second = send(down_half[half // 2 :], x_lane)
    down_mine = jnp.concatenate([down_first, down_second], 0)
    down_rest = send(down_mine, other_core)
    residual = (rows + gate1 * attn_sum).astype(jnp.bfloat16)
    second = norm_mod(residual.astype(jnp.float32), shift2, scale2)
    second = gather_z((second[:1], second[1:]))

    def feed(blocks):
        tokens = jnp.concatenate(blocks, 1)
        part = None
        for up, down in ((up_weight, down_weight), (up_mine, down_mine), (up_rest, down_rest)):
            hidden = jax.nn.gelu(
                jnp.einsum("jtd,df->jtf", tokens, up, preferred_element_type=jnp.float32),
                approximate=True,
            ).astype(jnp.bfloat16)
            more = jnp.einsum("jtf,fd->jtd", hold(hidden), down, preferred_element_type=jnp.float32)
            part = more if part is None else part + more
        part = part.astype(jnp.bfloat16)
        return jnp.split(part, len(blocks), 1)

    late = feed(second[5:])
    early = hold(tuple(second[:5]) + (late[-1],))
    ffn_sum = scatter_sum_z(feed(early[:5]) + late[:-1] + [early[5]])
    mixed = residual.astype(jnp.float32) + gate2 * ffn_sum
    return mixed.astype(jnp.bfloat16).transpose(1, 0, 2)


def solution(mesh):
    return jax.shard_map(
        body,
        mesh=mesh,
        in_specs=(
            P("space", "span", None),
            P(),
            P("span", None, None),
            P(None, None, "space"),
            P("space", None),
            P(None, "space"),
            P("space", None),
        ),
        out_specs=P("space", "span", None),
        check_vma=False,
    )
```
